128 devices in a mesh: dp: 64 (over x_hi, z, y, core), seq: 2 (over x_lo).
Axes of the slice: x: 4 (x_hi: 2, x_lo: 2; x = x_hi * 2 + x_lo), y: 4, z: 4, core: 2. Of those that a mesh axis runs over, the one named last changes fastest.
Arguments:
- hidden_in: bfloat16 [64, 512, 768], P('dp', 'seq'), may hold values from -6 to 6
- segment_ids: int32 [64, 512], P('dp', 'seq'), may hold values from 0 to 7, as said below
- out_cotangent: bfloat16 [64, 512, 768], P('dp', 'seq'), may hold values from -6 to 6
- qkv_weight: float32 [768, 2304], P(('dp', 'seq')), may hold values from -0.21875 to 0.21875
- qkv_moment: float32 [768, 2304], P(('dp', 'seq')), may hold values from -64 to 64
- qkv_square: float32 [768, 2304], P(('dp', 'seq')), may hold values from 4.096 to 65.536
- out_weight: float32 [768, 768], P(('dp', 'seq')), may hold values from -0.875 to 0.875
- out_moment: float32 [768, 768], P(('dp', 'seq')), may hold values from -64 to 64
- out_square: float32 [768, 768], P(('dp', 'seq')), may hold values from 4.096 to 65.536
- up_weight: float32 [768, 3072], P(('dp', 'seq')), may hold values from -0.21875 to 0.21875
- up_moment: float32 [768, 3072], P(('dp', 'seq')), may hold values from -64 to 64
- up_square: float32 [768, 3072], P(('dp', 'seq')), may hold values from 4.096 to 65.536
- down_weight: float32 [3072, 768], P(('dp', 'seq')), may hold values from -0.109375 to 0.109375
- down_moment: float32 [3072, 768], P(('dp', 'seq')), may hold values from -64 to 64
- down_square: float32 [3072, 768], P(('dp', 'seq')), may hold values from 4.096 to 65.536
- small_params: float32 [9216], P(('dp', 'seq')), may hold values from -1.2 to 1.4
- small_moment: float32 [9216], P(('dp', 'seq')), may hold values from -128 to 128
- small_square: float32 [9216], P(('dp', 'seq')), may hold values from 16.384 to 262.144
Outputs:
- layer_out: bfloat16 [64, 512, 768], P('dp', 'seq')
- input_grad: bfloat16 [64, 512, 768], P('dp', 'seq')
- qkv_master: float32 [768, 2304], P(('dp', 'seq'))
- qkv_momentum: float32 [768, 2304], P(('dp', 'seq'))
- qkv_squares: float32 [768, 2304], P(('dp', 'seq'))
- out_master: float32 [768, 768], P(('dp', 'seq'))
- out_momentum: float32 [768, 768], P(('dp', 'seq'))
- out_squares: float32 [768, 768], P(('dp', 'seq'))
- up_master: float32 [768, 3072], P(('dp', 'seq'))
- up_momentum: float32 [768, 3072], P(('dp', 'seq'))
- up_squares: float32 [768, 3072], P(('dp', 'seq'))
- down_master: float32 [3072, 768], P(('dp', 'seq'))
- down_momentum: float32 [3072, 768], P(('dp', 'seq'))
- down_squares: float32 [3072, 768], P(('dp', 'seq'))
- small_master: float32 [9216], P(('dp', 'seq'))
- small_momentum: float32 [9216], P(('dp', 'seq'))
- small_squares: float32 [9216], P(('dp', 'seq'))
The draws below stay inside these ranges and needn't reach their ends.
Inputs may be any that keep to these rules, and one draw needn't show every extreme that they name: `segment_ids`: along each row the numbers start at 0, never fall and rise by at most 1 from one token to the next; every row's last token has number 7; the tokens at places 256 - 1 and 256 of a row share a number.
All inputs are finite; a program needn't handle non-finite values.
Results may differ from the reference program's by a relative error of at most 0.012.
The reference program's roundings to bfloat16 on the way count: a program that leaves them out, or rounds other values in their place, can miss the bound.
Values may be sent and summed in bfloat16 or wider, within the bound.
No kernel may reach another device: no remote copies, remote signals or barrier semaphores. Data moves between devices by JAX's collectives and lax.ppermute only.
A program may use at most 192 MiB of HBM per device.

```python
import math
import jax
import jax.numpy as jnp
from jax import lax

D = 768
HEADS = 12
FF = 3072
TOK_DEV = 256
STEP = 10
LEN = 512
ROWS = 64
TOKENS = 32768
SMALL = 9216


def draw_segment_ids(key, part):
    key = jax.random.fold_in(key, 11)
    spacing = max(TOK_DEV // 4, 2)
    boundaries = LEN // spacing - 1
    candidates = lax.iota(jnp.int32, LEN - 2) + 1
    candidates = jnp.where(candidates >= TOK_DEV, candidates + 1, candidates).astype(jnp.int32)
    row_keys = jax.random.split(key, ROWS)
    shuffled = jax.vmap(lambda row_key: jax.random.permutation(row_key, candidates))(row_keys)
    chosen = shuffled[:, :boundaries]
    column = lax.iota(jnp.int32, LEN)
    starts = jnp.sum((column[None, None, :] == chosen[:, :, None]).astype(jnp.int32), axis=1)
    return jnp.cumsum(starts, axis=1).astype(jnp.int32)


def draw_small_params(key, part):
    key = jax.random.fold_in(key, 23)
    position = lax.iota(jnp.int32, 8 * D + FF)
    block_number = position // D
    is_gain = (block_number == 0) | (block_number == 5)
    noise = jnp.clip(jax.random.normal(key, (8 * D + FF,), jnp.float32), -4.0, 4.0)
    return jnp.where(is_gain, 1.0 + 0.1 * noise, 0.3 * noise)


def shard_levels(rng, extent, cuts, least, largest):
    def one(dim, shards_of):
        draws = jax.random.uniform(jax.random.fold_in(jax.random.fold_in(rng, 6), dim), (shards_of,), jnp.float32, least / len(cuts), largest / len(cuts))
        return jnp.repeat(jnp.exp(draws), extent[dim] // shards_of).reshape((-1,) + (1,) * (len(extent) - dim - 1))

    level = one(*cuts[0])
    for cut in cuts[1:]:
        level = level * one(*cut)
    return level


def normal_values(own_key, shape, scale, most, cuts=(), held_as=jnp.bfloat16):
    values = scale * jax.random.normal(own_key, shape, jnp.float32)
    if cuts:
        values = values * shard_levels(own_key, shape, cuts, -0.22, 0.18)
    return jnp.clip(values, -most, most).astype(held_as)


def setup_inputs(seed: int = 0) -> dict:
    streams_of = jax.random.split(jax.random.key(seed), 19)
    return {
        "hidden_in": normal_values(streams_of[0], (ROWS, LEN, D), 1.0, 6.0, ((0, 64), (1, 2))),
        "segment_ids": draw_segment_ids(jax.random.fold_in(streams_of[18], 71), 0),
        "out_cotangent": normal_values(streams_of[2], (ROWS, LEN, D), 1.0, 6.0, ((0, 64), (1, 2))),
        "qkv_weight": normal_values(streams_of[3], (D, 3 * D), D ** -0.5, 0.21875, ((0, 128),), jnp.float32),
        "qkv_moment": normal_values(streams_of[4], (D, 3 * D), (0.055 * TOKENS ** 0.5), 64.0, ((0, 128),), jnp.float32),
        "qkv_square": jnp.clip(jnp.exp(math.log(65.536) - 2.7725887 * jax.random.uniform(streams_of[5], (D, 3 * D), jnp.float32) ** shard_levels(streams_of[5], (D, 3 * D), ((0, 128),), -0.2, 0.2)), 4.096, 65.536),
        "out_weight": normal_values(streams_of[6], (D, D), (D // 16) ** -0.5, 0.875, ((0, 128),), jnp.float32),
        "out_moment": normal_values(streams_of[7], (D, D), (0.055 * TOKENS ** 0.5), 64.0, ((0, 128),), jnp.float32),
        "out_square": jnp.clip(jnp.exp(math.log(65.536) - 2.7725887 * jax.random.uniform(streams_of[8], (D, D), jnp.float32) ** shard_levels(streams_of[8], (D, D), ((0, 128),), -0.2, 0.2)), 4.096, 65.536),
        "up_weight": normal_values(streams_of[9], (D, FF), D ** -0.5, 0.21875, ((0, 128),), jnp.float32),
        "up_moment": normal_values(streams_of[10], (D, FF), (0.055 * TOKENS ** 0.5), 64.0, ((0, 128),), jnp.float32),
        "up_square": jnp.clip(jnp.exp(math.log(65.536) - 2.7725887 * jax.random.uniform(streams_of[11], (D, FF), jnp.float32) ** shard_levels(streams_of[11], (D, FF), ((0, 128),), -0.2, 0.2)), 4.096, 65.536),
        "down_weight": normal_values(streams_of[12], (FF, D), FF ** -0.5, 0.109375, ((0, 128),), jnp.float32),
        "down_moment": normal_values(streams_of[13], (FF, D), (0.055 * TOKENS ** 0.5), 64.0, ((0, 128),), jnp.float32),
        "down_square": jnp.clip(jnp.exp(math.log(65.536) - 2.7725887 * jax.random.uniform(streams_of[14], (FF, D), jnp.float32) ** shard_levels(streams_of[14], (FF, D), ((0, 128),), -0.2, 0.2)), 4.096, 65.536),
        "small_params": draw_small_params(jax.random.fold_in(streams_of[18], 71), 0),
        "small_moment": normal_values(streams_of[16], (SMALL,), (0.11 * TOKENS ** 0.5), 128.0, ((0, 128),), jnp.float32),
        "small_square": jnp.clip(jnp.exp(math.log(262.144) - 2.7725887 * jax.random.uniform(streams_of[17], (SMALL,), jnp.float32) ** shard_levels(streams_of[17], (SMALL,), ((0, 128),), -0.2, 0.2)), 16.384, 262.144),
    }


NORM_EPS = 1e-05
BETA_ONE = 0.9
BETA_TWO = 0.999
ADAM_EPS = 1e-08
MATRIX_RATE = 0.03
MATRIX_DECAY = 0.01
SMALL_RATE = 0.3
MASKED = -1e+30

@jax.custom_vjp
def low(v):
    return lax.optimization_barrier(v.astype(jnp.bfloat16)).astype(jnp.float32)

@jax.custom_vjp
def low_back(v):
    return v

def low_keep(v):
    return (low(v), None)

def low_pass(kept, grad):
    return (grad,)

def back_keep(v):
    return (v, None)

def back_low(kept, grad):
    return (low(grad),)
low.defvjp(low_keep, low_pass)
low_back.defvjp(back_keep, back_low)

def layer_norm(values, norm_gain, offset):
    center = values - lax.optimization_barrier(jnp.mean(values, axis=-1, keepdims=True))
    spread = lax.optimization_barrier(jnp.mean(center * center, axis=-1, keepdims=True))
    return center * lax.rsqrt(spread + NORM_EPS) * norm_gain + offset

def exact_dot(left, right):
    return jnp.dot(left, right, precision=lax.Precision.HIGHEST)

def split_small(small_vals, model_width, hidden_width):
    pieces = [small_vals[piece_index * model_width:(piece_index + 1) * model_width] for piece_index in range(8)]
    return pieces + [small_vals[8 * model_width:8 * model_width + hidden_width]]

def adam_update(master, moment, square, gradient, step_rate, decay_rate, step_count):
    moment_new = BETA_ONE * moment + (1.0 - BETA_ONE) * gradient
    square_new = BETA_TWO * square + (1.0 - BETA_TWO) * gradient * gradient
    moment_hat = moment_new / (1.0 - BETA_ONE ** step_count)
    square_hat = square_new / (1.0 - BETA_TWO ** step_count)
    master_new = master - step_rate * (moment_hat / (jnp.sqrt(square_hat) + ADAM_EPS) + decay_rate * master)
    return (master_new, moment_new, square_new)

def forward_row(qkv_full, out_full, up_full, down_full, small_vals, tokens, segments):
    model_width = out_full.shape[1]
    hidden_width = up_full.shape[1]
    row_length = tokens.shape[0]
    head_size = model_width // HEADS
    scaling = 1.0 / math.sqrt(head_size)
    gain_one, bias_one, query_bias, value_bias, out_bias, gain_two, bias_two, down_bias, up_bias = split_small(small_vals, model_width, hidden_width)
    normed_one = low(layer_norm(tokens, gain_one, bias_one))
    projected = exact_dot(normed_one, qkv_full)
    queries = low_back(low(projected[:, :model_width] + query_bias))
    key_rows = low_back(low(projected[:, model_width:2 * model_width]))
    values = low_back(low(projected[:, 2 * model_width:] + value_bias))
    query_heads = queries.reshape(row_length, HEADS, head_size)
    key_heads = key_rows.reshape(row_length, HEADS, head_size)
    value_heads = values.reshape(row_length, HEADS, head_size)
    scores = low_back(jnp.einsum('qhd,khd->hqk', query_heads, key_heads, precision=lax.Precision.HIGHEST) * scaling)
    position = lax.iota(jnp.int32, row_length)
    allowed = (segments[None, :] == segments[:, None]) & (position[None, :] <= position[:, None])
    attn_probs = jax.nn.softmax(jnp.where(allowed[None], scores, MASKED), axis=-1)
    mixed = jnp.einsum('hqk,khd->qhd', low(attn_probs), value_heads, precision=lax.Precision.HIGHEST)
    context = low_back(low(mixed.reshape(row_length, model_width)))
    attended = low_back(exact_dot(context, out_full) + out_bias)
    middle = tokens + attended
    normed_two = low(layer_norm(middle, gain_two, bias_two))
    pre_act = low_back(exact_dot(normed_two, up_full) + up_bias)
    activated = low(jax.nn.gelu(pre_act))
    return middle + exact_dot(activated, down_full) + down_bias

def reference(hidden_in, segment_ids, out_cotangent, qkv_weight, qkv_moment, qkv_square, out_weight, out_moment, out_square, up_weight, up_moment, up_square, down_weight, down_moment, down_square, small_params, small_moment, small_square):
    params = tuple((param.astype(jnp.bfloat16).astype(jnp.float32) for param in (qkv_weight, out_weight, up_weight, down_weight, small_params)))

    def one_row(carried, inputs):
        tokens, segments, upstream = inputs

        def row_forward(qkv_full, out_full, up_full, down_full, small_vals, token_rows):
            return forward_row(qkv_full, out_full, up_full, down_full, small_vals, token_rows, segments)
        result, backward = jax.vjp(row_forward, params[0], params[1], params[2], params[3], params[4], tokens)
        grads = backward(upstream)
        summed = tuple((total + part_grad for total, part_grad in zip(carried, grads[:5])))
        return (summed, (result.astype(jnp.bfloat16), grads[5].astype(jnp.bfloat16)))
    zero_grads = tuple((jnp.zeros_like(param) for param in params))
    totals, outputs = lax.scan(one_row, zero_grads, (hidden_in.astype(jnp.float32), segment_ids, out_cotangent.astype(jnp.float32)))
    layer_out, input_grad = outputs
    qkv_new = adam_update(qkv_weight, qkv_moment, qkv_square, totals[0], MATRIX_RATE, MATRIX_DECAY, STEP)
    out_new = adam_update(out_weight, out_moment, out_square, totals[1], MATRIX_RATE, MATRIX_DECAY, STEP)
    up_new = adam_update(up_weight, up_moment, up_square, totals[2], MATRIX_RATE, MATRIX_DECAY, STEP)
    down_new = adam_update(down_weight, down_moment, down_square, totals[3], MATRIX_RATE, MATRIX_DECAY, STEP)
    small_new = adam_update(small_params, small_moment, small_square, totals[4], SMALL_RATE, 0.0, STEP)
    return (layer_out, input_grad, qkv_new[0], qkv_new[1], qkv_new[2], out_new[0], out_new[1], out_new[2], up_new[0], up_new[1], up_new[2], down_new[0], down_new[1], down_new[2], small_new[0], small_new[1], small_new[2])
```

```python
import functools
import math

import jax
import jax.numpy as jnp
from jax import lax
from jax.experimental import pallas as pl
from jax.experimental.pallas import tpu as pltpu
from jax.sharding import Mesh
from jax.sharding import PartitionSpec as P

HEADS = 12
STEP = 10


NORM_EPS = 1e-05
BETA_ONE = 0.9
BETA_TWO = 0.999
ADAM_EPS = 1e-08
MATRIX_RATE = 0.03
MATRIX_DECAY = 0.01
SMALL_RATE = 0.3
MASKED = -1e30
GELU_SCALE = math.sqrt(2.0 / math.pi)
GELU_CUBE = 0.044715
VMEM_BYTES = 56 * 1024 * 1024

BF16 = jnp.bfloat16
F32 = jnp.float32


def shifted_by(value, axis, steps):
    count = lax.axis_size(axis)
    return lax.ppermute(value, axis, [(k, (k + steps) % count) for k in range(count)])


def swapped(value, axes):
    count = lax.axis_size(axes)
    return lax.ppermute(value, axes, [(k, count - 1 - k) for k in range(count)])


def ring_pieces(value, axis):
    return [value] + [shifted_by(value, axis, r) for r in range(1, lax.axis_size(axis))]


def placed(pieces, axis, dim):
    count = len(pieces)
    me = lax.axis_index(axis)
    shape = list(pieces[0].shape)
    shape.insert(dim, count)
    total = jnp.zeros(shape, pieces[0].dtype)
    for r, piece in enumerate(pieces):
        total = lax.dynamic_update_index_in_dim(total, piece, (me - r) % count, dim)
    return total


def half_of(value, which):
    width = value.shape[-1] // 2
    return lax.dynamic_slice_in_dim(value, which * width, width, value.ndim - 1)


def pair_parts(keep, other):
    return keep, swapped(keep, "s"), swapped(other, "c"), swapped(other, ("c", "s"))


def together(*groups):
    return lax.optimization_barrier(groups)


def gather_start(first, last, visitors):
    width = first.shape[1] * 2 // 5
    first, last, visitors = together(
        ring_pieces(first, "y"), ring_pieces(last, "xh"), swapped(visitors, "s")
    )
    first = placed(first, "y", 0)
    one, two, last = first[..., :width], first[..., width:], placed(last, "xh", 0)
    one, two, last = together(one, two, last)
    one, two, last = together(ring_pieces(one, "z"), ring_pieces(two, "xh"), last)
    one, two = placed(one, "z", 0), placed(two, "xh", 0)
    return (*together(one, two, last), visitors)


def fold(terms, axis, dim, start=0, stop=None):
    count, me = lax.axis_size(axis), lax.axis_index(axis)
    blocks = []
    for r in range(count):
        parts = []
        for t in terms:
            at = [0] * t.ndim
            at[dim], at[-1] = (me + r) % count, start
            sizes = list(t.shape)
            sizes[dim], sizes[-1] = 1, (stop or t.shape[-1]) - start
            parts.append(jnp.squeeze(lax.dynamic_slice(t, at, sizes), dim))
        blocks.append(sum(p.astype(jnp.float32) for p in parts).astype(jnp.bfloat16))
    return blocks


def sent(blocks, axis):
    return [blocks[0]] + [shifted_by(blocks[r], axis, r) for r in range(1, len(blocks))]


def over_core(keep, send):
    shape = (2, 4, 4, keep.shape[0] // 32, keep.shape[1])
    return [keep.reshape(shape), swapped(send, "c").reshape(shape)]


def chip_pair_fold(total):
    core, side = lax.axis_index("c"), lax.axis_index("s")
    total = total.reshape((2, 2, total.shape[0] // 4) + total.shape[1:])

    def rows_of(k):
        at = ((core + k // 2) % 2, (side + k % 2) % 2) + (0,) * (total.ndim - 2)
        return lax.dynamic_slice(total, at, (1, 1) + total.shape[2:])[0, 0]

    def arrived(k, axes):
        return swapped(rows_of(k).astype(jnp.bfloat16), axes).astype(jnp.float32)

    mine = rows_of(0) + arrived(1, "s")
    theirs = arrived(2, "c") + arrived(3, ("c", "s"))
    return mine, theirs


def rejoined(pair, start, stop):
    core = lax.axis_index("c")
    mine, theirs = pair[0][:, start:stop], pair[1][:, start:stop]
    return jnp.concatenate(
        [jnp.where(core == 0, mine, theirs), jnp.where(core == 0, theirs, mine)], axis=1
    )


def adam_update(master, moment, square, gradient, step_rate, decay_rate, step_count):
    moment_new = BETA_ONE * moment + (1.0 - BETA_ONE) * gradient
    square_new = BETA_TWO * square + (1.0 - BETA_TWO) * gradient * gradient
    moment_hat = moment_new / (1.0 - BETA_ONE**step_count)
    square_hat = square_new / (1.0 - BETA_TWO**step_count)
    master_new = master - step_rate * (
        moment_hat / (jnp.sqrt(square_hat) + ADAM_EPS) + decay_rate * master
    )
    return (master_new, moment_new, square_new)


def dot_nn(left, right):
    return jnp.dot(left, right, preferred_element_type=F32)


def dot_nt(left, right):
    return lax.dot_general(left, right, (((1,), (1,)), ((), ())), preferred_element_type=F32)


def turned(values):
    return values.astype(F32).T


def lanes(start, size):
    return pl.ds(pl.multiple_of(start, 128), size)


def rows(start, size):
    return pl.ds(pl.multiple_of(start, size), size)


def weights_of(place_ref, pieces, mine_ref, theirs_ref):
    count = len(pieces) // 2
    inner = pieces[0].shape[0]
    size = pieces[0].shape[1]
    for target, group in ((mine_ref, pieces[:count]), (theirs_ref, pieces[count:])):
        for r, piece in enumerate(group):
            at = lax.rem(place_ref[1] - r + count, count)
            for part in range(inner):
                target[rows((part * count + at) * size, size), :] = piece[part]


def column_sum(values):
    return jnp.sum(values, axis=0, keepdims=True)


def line_masks(width, lane_count):
    per_row = 12
    group = width // per_row
    place = lax.broadcasted_iota(jnp.int32, (group, width), 1)
    row = lax.broadcasted_iota(jnp.int32, (group, width), 0)
    lane = lax.broadcasted_iota(jnp.int32, (width, lane_count), 1)
    start = lax.broadcasted_iota(jnp.int32, (width, lane_count), 0)
    inside = (place >= row * per_row) & (place < (row + 1) * per_row)
    pick = jnp.where(lax.rem(start, per_row) == lane, 1.0, 0.0).astype(BF16)
    return inside, pick


def norm_parts(values):
    center = values - jnp.mean(values, axis=-1, keepdims=True)
    spread = jnp.mean(center * center, axis=-1, keepdims=True)
    inverse = lax.rsqrt(spread + NORM_EPS)
    return center * inverse, inverse


def norm_pull(grad, hat, inverse, gain):
    scaled = gain * grad
    shift = jnp.mean(scaled, axis=-1, keepdims=True)
    slope = jnp.mean(scaled * hat, axis=-1, keepdims=True)
    return (scaled - shift - hat * slope) * inverse


def pack_kernel(place_ref, qkv_ref, small_ref, up_ref, out_ref, down_ref, keep_ref, other_ref):
    core = place_ref[0]
    for which, target in ((core, keep_ref), (1 - core, other_ref)):
        at = 0
        for source in (qkv_ref, small_ref, up_ref, out_ref):
            if source is small_ref:
                inside, pick = line_masks(source.shape[1], 128)
                line = jnp.where(inside, source[...], 0.0).astype(BF16)
                target[:, at : at + 128] = dot_nn(line, pick).astype(BF16)
                at += 128
                continue
            half = source.shape[1] // 2
            target[:, at : at + half] = source[:, lanes(which * half, half)].astype(BF16)
            at += half
        half = down_ref.shape[1] // 2
        count = target.shape[0]
        for part in range(down_ref.shape[0] // count):
            block = down_ref[part * count : (part + 1) * count, lanes(which * half, half)]
            target[:, at : at + half] = block.astype(BF16)
            at += half


def unpack_kernel(place_ref, *refs):
    parts, (first_ref, last_ref) = refs[:4], refs[4:]
    me = 2 * place_ref[0] + place_ref[1]
    count = parts[0].shape[0]
    width, half = first_ref.shape[1], last_ref.shape[1]
    values = [part[...].astype(F32) for part in parts]
    rows_first, rows_last = [], []
    for t in range(4):
        value = values[0]
        for k in range(1, 4):
            value = jnp.where(me == t ^ k, values[k], value)
        rows_first.append(value[:, :width])
        for at in range(width, value.shape[1], half):
            rows_last.append(value[:, at : at + half])
    first_ref[...] = jnp.concatenate(rows_first, axis=0).astype(BF16)
    last_ref[...] = jnp.concatenate(rows_last, axis=0).astype(BF16)


def segment_bias(own_ref, before_ref, late, width):
    own = own_ref.shape[0]
    total = 2 * own
    seg_own = own_ref[:, width:].astype(F32)
    seg_before = before_ref[:, width:].astype(F32)
    seg_before = jnp.where(late > 0, seg_before, -1.0)
    seg_k = jnp.concatenate([seg_before[:, 0:1], seg_own[:, 0:1]], axis=0)
    place_q = lax.broadcasted_iota(jnp.int32, (total, own), 1) + own
    place_k = lax.broadcasted_iota(jnp.int32, (total, own), 0)
    allowed = (seg_k == seg_own.T[0:1]) & (place_k <= place_q)
    return jnp.where(allowed, 0.0, MASKED)


def attend_kernel(core_ref, own_ref, before_ref, *refs):
    pieces = refs[:4]
    (
        turned_ref, q_ref, k_ref, v_ref, ctx_ref, ctx_turned_ref, lse_ref, vec_ref,
        normed_ref, proj_ref, bias_ref, mine_ref, theirs_ref,
    ) = refs[4:]
    weights_of(core_ref, pieces, mine_ref, theirs_ref)
    core = core_ref[0]
    span = mine_ref.shape[1] - 128
    inside, pick = line_masks(q_ref.shape[1], 128)
    group = inside.shape[0]
    for r in range(vec_ref.shape[0]):
        lines = dot_nt(mine_ref[r * group : (r + 1) * group, span:], pick)
        vec_ref[r : r + 1, :] = column_sum(jnp.where(inside, lines, 0.0))
    own, width = q_ref.shape
    total = 2 * own
    half = proj_ref.shape[1] // 2
    tile = 384

    for source, base in ((before_ref, 0), (own_ref, own)):
        for part in range(0, own, 128):
            hat, _ = norm_parts(source[part : part + 128, :width].astype(F32))
            normed = hat * vec_ref[0:1, :] + vec_ref[1:2, :]
            normed_ref[base + part : base + part + 128, :] = normed.astype(BF16)
            turned_ref[:, base + part : base + part + 128] = turned(normed).astype(BF16)

    def proj_step(t, carry):
        normed = normed_ref[...]
        proj_ref[:, lanes(core * half + t * tile, tile)] = dot_nn(
            normed, mine_ref[:, lanes(t * tile, tile)]
        )
        proj_ref[:, lanes((1 - core) * half + t * tile, tile)] = dot_nn(
            normed, theirs_ref[:, lanes(t * tile, tile)]
        )
        return carry

    lax.fori_loop(0, half // tile, proj_step, 0)

    bias_ref[...] = segment_bias(own_ref, before_ref, core_ref[2], width)
    lane_row = lax.broadcasted_iota(jnp.int32, (1, 128), 1)

    def pair_step(j, carry):
        at = lanes(j * 128, 128)
        q = (proj_ref[total - own :, at] + vec_ref[2:3, at]).astype(BF16)
        k = proj_ref[:, lanes(width + j * 128, 128)].astype(BF16)
        v = (proj_ref[:, lanes(2 * width + j * 128, 128)] + vec_ref[3:4, at]).astype(BF16)
        q_ref[:, at] = q
        k_ref[:, at] = k
        v_ref[:, at] = v
        v_turned = turned(v).astype(BF16)
        outs = []
        for h in range(2):
            head_lanes = jnp.where(lane_row // 64 == h, 1.0, 0.0).astype(BF16)
            scores = dot_nt(k, q * head_lanes) * 0.125 + bias_ref[...]
            top = jnp.max(scores, axis=0, keepdims=True)
            weights = jnp.exp(scores - top)
            mass = jnp.sum(weights, axis=0, keepdims=True)
            probs = (weights * (1.0 / mass)).astype(BF16)
            outs.append(dot_nn(v_turned[h * 64 : (h + 1) * 64], probs))
            lse_ref[pl.ds(2 * j + h, 1), :] = top + jnp.log(mass)
        mixed = jnp.concatenate(outs, axis=0)
        ctx_turned_ref[rows(j * 128, 128), :] = mixed.astype(BF16)
        ctx_ref[:, at] = mixed.T.astype(BF16)
        return carry

    lax.fori_loop(0, HEADS // 2, pair_step, 0)


def up_kernel(
    core_ref, hid_ref, ctx_ref, vec_ref, *refs
):
    pieces = refs[:8]
    (
        mid_ref, turned_ref, act_ref, act_turned_ref, slope_ref,
        normed_ref, mine_ref, theirs_ref,
    ) = refs[8:]
    weights_of(core_ref, pieces, mine_ref, theirs_ref)
    core = core_ref[0]
    width = hid_ref.shape[1]
    ff_half = act_ref.shape[1] // 2
    half = width // 2
    tile = 512
    ctx = ctx_ref[...]
    for which, ref in ((core, mine_ref), (1 - core, theirs_ref)):
        at = lanes(which * half, half)
        mid_ref[:, at] = (
            hid_ref[:, at].astype(F32)
            + (dot_nn(ctx, ref[:, ff_half : ff_half + half]) + vec_ref[4:5, at])
        )
    hat, _ = norm_parts(mid_ref[...])
    normed = hat * vec_ref[5:6, :] + vec_ref[6:7, :]
    normed_ref[...] = normed.astype(BF16)
    turned_ref[...] = turned(normed).astype(BF16)

    def up_step(t, carry):
        for which, ref in ((core, mine_ref), (1 - core, theirs_ref)):
            base = which * ff_half + t * tile
            pre = dot_nn(normed_ref[...], ref[:, lanes(t * tile, tile)])
            for part in range(tile // 256):
                at = base + part * 256
                u = pre[:, part * 256 : (part + 1) * 256] + vec_ref[
                    pl.ds(8 + at // width, 1), lanes(at % width, 256)
                ]
                square = u * u
                tanh = jnp.tanh(GELU_SCALE * (u + GELU_CUBE * (square * u)))
                act = 0.5 * u * (1.0 + tanh)
                act_ref[:, lanes(at, 256)] = act.astype(BF16)
                act_turned_ref[rows(at, 256), :] = turned(act).astype(BF16)
                slope_ref[:, lanes(at, 256)] = 0.5 * (1.0 + tanh) + (0.5 * GELU_SCALE) * u * (
                    1.0 - tanh * tanh
                ) * (1.0 + (3.0 * GELU_CUBE) * square)
        return carry

    lax.fori_loop(0, ff_half // tile, up_step, 0)


def down_kernel(core_ref, act_ref, grad_ref, keep_ref, send_ref):
    core = core_ref[0]
    half = grad_ref.shape[1] // 2
    tile = 512
    grads = jnp.concatenate(
        [grad_ref[:, lanes(core * half, half)], grad_ref[:, lanes((1 - core) * half, half)]], axis=1
    )

    def down_step(t, carry):
        at = rows(t * tile, tile)
        both = dot_nn(act_ref[at, :], grads).astype(BF16)
        keep_ref[at, :] = both[:, :half]
        send_ref[at, :] = both[:, half:]
        return carry

    lax.fori_loop(0, act_ref.shape[0] // tile, down_step, 0)


def middle_kernel(
    core_ref, normed_ref, slope_ref, grad_ref, *refs
):
    pieces = refs[:8]
    dpre_ref, send_ref, small_ref, down_mine_ref, down_theirs_ref = refs[8:]
    weights_of(core_ref, pieces, down_mine_ref, down_theirs_ref)
    core = core_ref[0]
    width = normed_ref.shape[0]
    ff_half = slope_ref.shape[1] // 2
    half = width // 2
    tile = 512
    sides = ((core, down_mine_ref), (1 - core, down_theirs_ref))

    small_ref[0:1, :] = column_sum(grad_ref[...].astype(F32))

    def pre_step(t, carry):
        at = t * 256
        grad_act = sum(
            dot_nt(grad_ref[:, lanes(which * half, half)], down[rows(at, 256), :])
            for which, down in sides
        )
        pre = (grad_act * slope_ref[:, lanes(at, 256)]).astype(BF16)
        dpre_ref[:, lanes(at, 256)] = pre
        small_ref[pl.ds(1 + at // width, 1), lanes(at % width, 256)] = column_sum(pre.astype(F32))
        return carry

    lax.fori_loop(0, 2 * ff_half // 256, pre_step, 0)

    def weight_step(t, carry):
        pre = dpre_ref[:, lanes((1 - core) * ff_half + t * tile, tile)]
        send_ref[:, lanes(t * tile, tile)] = dot_nn(normed_ref[...], pre).astype(BF16)
        return carry

    lax.fori_loop(0, ff_half // tile, weight_step, 0)


def keep_kernel(core_ref, normed_ref, dpre_ref, keep_ref):
    core = core_ref[0]
    ff_half = dpre_ref.shape[1] // 2
    tile = 512

    def weight_step(t, carry):
        pre = dpre_ref[:, lanes(core * ff_half + t * tile, tile)]
        keep_ref[:, lanes(t * tile, tile)] = dot_nn(normed_ref[...], pre).astype(BF16)
        return carry

    lax.fori_loop(0, ff_half // tile, weight_step, 0)


def output_kernel(core_ref, mid_ref, act_ref, vec_ref, *refs):
    pieces = refs[:8]
    out_ref, mine_ref, theirs_ref = refs[8:]
    weights_of(core_ref, pieces, mine_ref, theirs_ref)
    core = core_ref[0]
    half = mid_ref.shape[1] // 2
    for which, down in ((core, mine_ref), (1 - core, theirs_ref)):
        at = lanes(which * half, half)
        out_ref[:, at] = (
            mid_ref[:, at] + dot_nn(act_ref[...], down[...]) + vec_ref[7:8, at]
        ).astype(BF16)


def context_kernel(
    core_ref, mid_ref, grad_ref, ctx_ref, vec_ref, dpre_ref, *refs
):
    pieces = refs[:8]
    dmid_ref, dctx_ref, keep_ref, send_ref, small_ref, work_ref, mine_ref, theirs_ref = refs[8:]
    weights_of(core_ref, pieces, mine_ref, theirs_ref)
    core = core_ref[0]
    width = mid_ref.shape[1]
    ff_half = dpre_ref.shape[1] // 2
    half = width // 2
    sides = ((core, mine_ref, keep_ref), (1 - core, theirs_ref, send_ref))

    def back_step(t, carry):
        at = t * 256
        work_ref[:, lanes(at, 256)] = sum(
            dot_nt(dpre_ref[:, lanes(which * ff_half, ff_half)], up[rows(at, 256), :ff_half])
            for which, up, _ in sides
        )
        return carry

    lax.fori_loop(0, width // 256, back_step, 0)

    grad_normed = work_ref[...]
    hat, inverse = norm_parts(mid_ref[...])
    small_ref[1:2, :] = column_sum(grad_normed * hat)
    small_ref[2:3, :] = column_sum(grad_normed)
    dmid = grad_ref[...].astype(F32) + norm_pull(grad_normed, hat, inverse, vec_ref[5:6, :])
    dmid_ref[...] = dmid
    small_ref[0:1, :] = column_sum(dmid.astype(BF16).astype(F32))

    ctx = ctx_ref[...]
    for which, _, target in sides:
        datt = dmid_ref[:, lanes(which * half, half)].astype(BF16)
        target[...] = dot_nn(ctx, datt).astype(BF16)

    def ctx_step(t, carry):
        at = t * 256
        dctx_ref[:, lanes(at, 256)] = sum(
            dot_nt(
                dmid_ref[:, lanes(which * half, half)].astype(BF16),
                out[rows(at, 256), ff_half : ff_half + half],
            )
            for which, out, _ in sides
        ).astype(BF16)
        return carry

    lax.fori_loop(0, width // 256, ctx_step, 0)


def first_kernel(
    core_ref, own_ref, before_ref,
    normed_ref, q_ref, k_ref, v_ref, lse_ref, dctx_ref,
    dproj_ref, send_ref, small_ref, bias_ref,
):
    core = core_ref[0]
    own, width = q_ref.shape
    total = normed_ref.shape[1]
    half = dproj_ref.shape[1] // 2
    tile = 384
    early = total - own

    bias_ref[...] = segment_bias(own_ref, before_ref, core_ref[2], width)
    dproj_ref[:early, :width] = jnp.zeros((early, width), BF16)
    lane_row = lax.broadcasted_iota(jnp.int32, (1, 128), 1)

    def pair_step(j, carry):
        at = lanes(j * 128, 128)
        q, k, v, dctx = q_ref[:, at], k_ref[:, at], v_ref[:, at], dctx_ref[:, at]
        k_turned = turned(k).astype(BF16)
        grad_q, grad_k, grad_v = [], [], []
        for h in range(2):
            head_lanes = jnp.where(lane_row // 64 == h, 1.0, 0.0).astype(BF16)
            q_head, dctx_head = q * head_lanes, dctx * head_lanes
            lse = lse_ref[pl.ds(2 * j + h, 1), :]
            probs = jnp.exp(dot_nt(k, q_head) * 0.125 + bias_ref[...] - lse)
            grad_probs = dot_nt(v, dctx_head)
            weighted = jnp.sum(probs * grad_probs, axis=0, keepdims=True)
            grad_scores = (probs * (grad_probs - weighted)).astype(BF16) * jnp.asarray(0.125, BF16)
            grad_q.append(dot_nn(k_turned[h * 64 : (h + 1) * 64], grad_scores))
            grad_k.append(dot_nn(grad_scores, q_head))
            grad_v.append(dot_nn(probs.astype(BF16), dctx_head))
        dq = jnp.concatenate(grad_q, axis=0).T.astype(BF16)
        dv = (grad_v[0] + grad_v[1]).astype(BF16)
        dproj_ref[early:, at] = dq
        dproj_ref[:, lanes(width + j * 128, 128)] = (grad_k[0] + grad_k[1]).astype(BF16)
        dproj_ref[:, lanes(2 * width + j * 128, 128)] = dv
        small_ref[0:1, at] = column_sum(dq.astype(F32))
        small_ref[1:2, at] = column_sum(dv.astype(F32))
        return carry

    lax.fori_loop(0, HEADS // 2, pair_step, 0)

    def weight_step(t, carry):
        normed = normed_ref[...]
        grads = dproj_ref[:, lanes((1 - core) * half + t * tile, tile)]
        send_ref[:, lanes(t * tile, tile)] = dot_nn(normed, grads).astype(BF16)
        return carry

    lax.fori_loop(0, half // tile, weight_step, 0)


def token_kernel(
    core_ref, own_ref, visit_ref, vec_ref, normed_ref, dproj_ref, dmid_ref, qv_ref, mid_small_ref,
    ff_small_ref, *refs
):
    pieces = refs[:4]
    (
        keep_ref, base_ref, before_ref, lines_ref,
        work_ref, mine_ref, theirs_ref, small_ref, spread_ref,
    ) = refs[4:]
    weights_of(core_ref, pieces, mine_ref, theirs_ref)
    core = core_ref[0]
    own, width = base_ref.shape
    early = own
    half = dproj_ref.shape[1] // 2
    sides = ((core, mine_ref), (1 - core, theirs_ref))
    tile = 384

    def weight_step(t, carry):
        grads = dproj_ref[:, lanes(core * half + t * tile, tile)]
        keep_ref[:, lanes(t * tile, tile)] = dot_nn(normed_ref[...], grads).astype(BF16)
        return carry

    lax.fori_loop(0, half // tile, weight_step, 0)

    def back_step(t, carry):
        at = t * 256
        work_ref[:, lanes(at, 256)] = sum(
            dot_nt(dproj_ref[:, lanes(which * half, half)], weight[rows(at, 256), :half])
            for which, weight in sides
        )
        return carry

    lax.fori_loop(0, width // 256, back_step, 0)

    grad_early = work_ref[:early, :]
    hat_early, _ = norm_parts(visit_ref[:, :width].astype(F32))
    before_ref[...] = grad_early.astype(BF16)
    grad_own = work_ref[early:, :]
    hat_own, inverse = norm_parts(own_ref[:, :width].astype(F32))
    small_ref[0:1, :] = column_sum(grad_early * hat_early) + column_sum(grad_own * hat_own)
    small_ref[1:2, :] = column_sum(grad_early) + column_sum(grad_own)
    base_ref[...] = dmid_ref[...] + norm_pull(grad_own, hat_own, inverse, vec_ref[0:1, :])
    at = 2
    for source in (qv_ref, mid_small_ref, ff_small_ref):
        small_ref[at : at + source.shape[0], :] = source[...]
        at += source.shape[0]
    inside, pick = line_masks(width, 128)
    group = inside.shape[0]
    for r in range(at):
        line = jnp.where(inside, small_ref[r : r + 1, :], 0.0)
        spread_ref[r * group : (r + 1) * group, :] = line.astype(BF16)
    lines_ref[...] = dot_nn(spread_ref[...], pick).astype(BF16)


def last_kernel(hid_ref, base_ref, later_ref, vec_ref, out_ref):
    hat, inverse = norm_parts(hid_ref[...].astype(F32))
    later = norm_pull(later_ref[...].astype(F32), hat, inverse, vec_ref[0:1, :])
    out_ref[...] = (base_ref[...] + later).astype(BF16)


def run(kernel, core, operands, outs, scratch=(), flops=0, name=None, moved=None):
    whole = pl.BlockSpec(memory_space=pltpu.VMEM)
    shapes = [jax.ShapeDtypeStruct(shape, dtype) for shape, dtype in outs]
    moved = moved or sum(a.size * a.dtype.itemsize for a in (*operands, *shapes))
    specs = [whole] * len(operands)
    if core is not None:
        operands = (core, *operands)
        specs = [pl.BlockSpec(memory_space=pltpu.SMEM)] + specs
    return pl.pallas_call(
        kernel,
        out_shape=shapes,
        in_specs=specs,
        out_specs=[whole] * len(shapes),
        scratch_shapes=[pltpu.VMEM(shape, dtype) for shape, dtype in scratch],
        compiler_params=pltpu.CompilerParams(vmem_limit_bytes=VMEM_BYTES),
        cost_estimate=pl.CostEstimate(flops=flops, bytes_accessed=moved, transcendentals=0),
        name=name,
    )(*operands)


def local(
    hidden_in,
    segment_ids,
    out_cotangent,
    qkv_weight,
    qkv_moment,
    qkv_square,
    out_weight,
    out_moment,
    out_square,
    up_weight,
    up_moment,
    up_square,
    down_weight,
    down_moment,
    down_square,
    small_params,
    small_moment,
    small_square,
):
    width = out_weight.shape[1]
    hidden = up_weight.shape[1]
    half, ff_half, third = width // 2, hidden // 2, qkv_weight.shape[1] // 2
    own = hidden_in.shape[1]
    tokens, upstream, seg_own = hidden_in[0], out_cotangent[0], segment_ids[0]
    core = lax.axis_index("c")
    core_of = core.astype(jnp.int32).reshape(1)

    def place(axis):
        return jnp.stack([core, lax.axis_index(axis), lax.axis_index("s")]).astype(jnp.int32)

    def shaped(pieces, inner):
        return [p.reshape(inner, -1, p.shape[-1]) for p in pieces]

    span = third + 128 + ff_half + half
    keep, other = run(
        pack_kernel,
        place("s"),
        (qkv_weight, small_params.reshape(1, -1), up_weight, out_weight, down_weight),
        [((6, span + 4 * half), BF16)] * 2,
        name="pack",
    )
    first, last = run(
        unpack_kernel,
        place("s"),
        pair_parts(keep, other),
        [((24, span), BF16), ((96, half), BF16)],
        name="unpack",
    )
    first, last, tokens_in, seg_in = together(first, last, tokens, seg_own)
    seg_line = jnp.broadcast_to(seg_in.astype(BF16)[:, None], (own, 128))
    own_lines = jnp.concatenate([tokens_in, seg_line], axis=1)
    one, two, last, visitors = gather_start(first, last, own_lines)

    one = ring_pieces(one, "xh")
    two = [two] + [shifted_by(two, "z", r) for r in (1, 3)]
    one_first, two_first = swapped(one[0], "c"), swapped(two[0], "c")
    one_first, last = together(one_first, last)
    last = ring_pieces(last, "z")
    one, one_first, two, two_first, last = together(one, one_first, two, two_first, last)
    last = placed(last, "z", 1)
    last_near = [shifted_by(last, "y", r) for r in (1, 3)]
    two_far = shifted_by(two[0], "z", 2)
    one = shaped(one + [one_first, swapped(one[1], "c")], 1)

    normed_one, queries, keys, values, context, context_turned, lse, vectors = run(
        attend_kernel,
        place("xh"),
        (own_lines, visitors, *one),
        [
            ((width, 2 * own), BF16), ((own, width), BF16), ((2 * own, width), BF16),
            ((2 * own, width), BF16), ((own, width), BF16), ((width, own), BF16),
            ((16, own), F32), ((12, width), F32),
        ],
        [
            ((2 * own, width), BF16),
            ((2 * own, 3 * width), F32), ((2 * own, own), F32),
            ((width, third + 128), BF16), ((width, third + 128), BF16),
        ],
        flops=12_000_000_000,
        name="attend",
    )
    two_theirs = [two_first, swapped(two[1], "c"), swapped(two[2], "c")]
    context, lse, two_far, two_theirs, last_near = together(
        context, lse, two_far, two_theirs, last_near
    )
    two = shaped(
        [two[0], two[1], two_far, two[2]]
        + [two_theirs[0], two_theirs[1], swapped(two_far, "c"), two_theirs[2]],
        2,
    )
    middle, normed_two, activated, act_turned, slope = run(
        up_kernel,
        place("z"),
        (tokens, context, vectors, *two),
        [
            ((own, width), F32), ((width, own), BF16), ((own, hidden), BF16),
            ((hidden, own), BF16), ((own, hidden), F32),
        ],
        [((own, width), BF16), ((width, ff_half + half), BF16), ((width, ff_half + half), BF16)],
        flops=9_000_000_000,
        name="up",
    )
    last_far = shifted_by(last, "y", 2)
    last_theirs = [swapped(p, "c") for p in (last, *last_near)]
    middle, act_turned, last_far, last_theirs = together(
        middle, act_turned, last_far, last_theirs
    )
    far_theirs = swapped(last_far, "c")
    down_keep, down_send = run(
        down_kernel,
        core_of,
        (act_turned, upstream),
        [((hidden, half), BF16), ((hidden, half), BF16)],
        flops=3_000_000_000,
        name="down",
    )
    down_keep, down_send, far_theirs = together(down_keep, down_send, far_theirs)
    last = [
        last, last_near[0], last_far, last_near[1],
        last_theirs[0], last_theirs[1], far_theirs, last_theirs[2],
    ]
    last = shaped(together(*last), 8)
    fold_down = over_core(down_keep, down_send)
    grad_pre, up_send, small_mid = run(
        middle_kernel,
        place("y"),
        (normed_two, slope, upstream, *last),
        [((own, hidden), BF16), ((width, ff_half), BF16), ((5, width), F32)],
        [((hidden, half), BF16), ((hidden, half), BF16)],
        flops=9_000_000_000,
        name="middle",
    )
    grad_pre, up_send, fold_down = together(grad_pre, up_send, fold_down)
    up_theirs = swapped(up_send, "c")
    blocks_down = fold(fold_down, "y", 2)
    grad_pre, blocks_down = together(grad_pre, blocks_down)
    sent_down = sent(blocks_down, "y")
    (up_keep,) = run(
        keep_kernel,
        core_of,
        (normed_two, grad_pre),
        [((width, ff_half), BF16)],
        flops=2_500_000_000,
        name="keep",
    )
    up_keep, up_theirs, grad_pre = together(up_keep, up_theirs, grad_pre)
    shape = (2, 4, 4, -1, ff_half)
    blocks_two = fold([up_keep.reshape(shape), up_theirs.reshape(shape)], "z", 1)
    blocks_two, grad_pre = together(blocks_two, grad_pre)
    two_near = [shifted_by(blocks_two[r], "z", r) for r in (1, 3)]
    grad_middle, grad_context, out_keep, out_send, small_ctx = run(
        context_kernel,
        place("z"),
        (middle, upstream, context_turned, vectors, grad_pre, *two),
        [
            ((own, width), F32), ((own, width), BF16), ((width, half), BF16),
            ((width, half), BF16), ((3, width), F32),
        ],
        [
            ((own, width), F32), ((width, ff_half + half), BF16),
            ((width, ff_half + half), BF16),
        ],
        flops=9_000_000_000,
        name="context",
    )
    grad_middle, grad_context, out_keep, out_send, sent_down, two_near, two_far = together(
        grad_middle, grad_context, out_keep, out_send, sent_down, two_near, blocks_two[2]
    )
    fold_out = over_core(out_keep, out_send)
    blocks_down = fold(sent_down, "xh", 0)
    blocks_down, grad_context = together(blocks_down, grad_context)
    two_far = shifted_by(two_far, "z", 2)
    sent_down = sent(blocks_down, "xh")
    grad_proj, one_send, small_qv = run(
        first_kernel,
        place("s"),
        (own_lines, visitors, normed_one, queries, keys, values, lse, grad_context),
        [((2 * own, 3 * width), BF16), ((width, third), BF16), ((2, width), F32)],
        [((2 * own, own), F32)],
        flops=15_000_000_000,
        name="first",
    )
    grad_proj, one_send, two_far, sent_down, fold_out = together(
        grad_proj, one_send, two_far, sent_down, fold_out
    )
    one_theirs = swapped(one_send, "c")
    blocks_two = fold([blocks_two[0], two_near[0], two_far, two_near[1]], "xh", 0)
    blocks_down = fold(sent_down, "z", 0)
    blocks_two, blocks_down, grad_proj = together(blocks_two, blocks_down, grad_proj)
    sent_two, sent_down = sent(blocks_two, "xh"), sent(blocks_down, "z")
    one_keep, base, before, small_lines = run(
        token_kernel,
        place("xh"),
        (
            own_lines, visitors, vectors, normed_one, grad_proj, grad_middle,
            small_qv, small_ctx, small_mid, *one,
        ),
        [
            ((width, third), BF16), ((own, width), F32), ((own, width), BF16),
            ((width, 128), BF16),
        ],
        [
            ((2 * own, width), F32), ((width, third + 128), BF16), ((width, third + 128), BF16),
            ((12, width), F32), ((width, width), BF16),
        ],
        flops=8_000_000_000,
        name="token",
    )
    one_keep, one_theirs, small_lines, before, sent_down, sent_two = together(
        one_keep, one_theirs, small_lines, before, sent_down, sent_two
    )
    shape = (2, 4, 4, -1, third)
    fold_one = [one_keep.reshape(shape), one_theirs.reshape(shape)]
    small_lines = small_lines.reshape(2, 4, 4, -1, 128)
    cut = half
    blocks_left = [
        jnp.concatenate(b, axis=-1)
        for b in zip(fold(fold_one, "xh", 0, 0, cut), fold(fold_out, "xh", 0))
    ]
    blocks_right = [
        jnp.concatenate(b, axis=-1)
        for b in zip(fold(fold_one, "y", 2, cut), fold([small_lines], "y", 2))
    ]
    blocks_left, blocks_right = together(blocks_left, blocks_right)
    sent_left, sent_right = sent(blocks_left, "xh"), sent(blocks_right, "y")
    sent_right[1], activated = together(sent_right[1], activated)
    (layer_out,) = run(
        output_kernel,
        place("y"),
        (middle, activated, vectors, *last),
        [((own, width), BF16)],
        [((hidden, half), BF16), ((hidden, half), BF16)],
        flops=3_000_000_000,
        name="output",
    )
    sent_left, sent_right, layer_out = together(sent_left, sent_right, layer_out)
    later = lax.ppermute(before, "s", [(1, 0)])
    sent_left = sent(fold(sent_left, "y", 1), "y")
    sent_right = sent(fold(sent_right, "xh", 0), "xh")
    sent_left, sent_right, later = together(sent_left, sent_right, later)
    blocks_one = [
        jnp.concatenate(b, axis=-1)
        for b in zip(fold(sent_left, "z", 0), fold(sent_right, "z", 0))
    ]
    sent_one = sent(blocks_one, "z")
    sent_two = sent(fold(sent_two, "y", 0), "y")
    (input_grad,) = run(
        last_kernel,
        None,
        (tokens, base, later, vectors),
        [((own, width), BF16)],
        flops=100_000_000,
        name="last",
    )
    sent_one, sent_two, input_grad = together(sent_one, sent_two, input_grad)
    down_total = sum(t.astype(F32) for t in sent_down).reshape(4, 4, 6, half)
    down_total = jnp.concatenate([down_total[:, k] for k in range(4)], axis=-1)
    total = jnp.concatenate(
        [sum(t.astype(F32) for t in g) for g in (sent_one, sent_two)]
        + [down_total.reshape(24, 4 * half)],
        axis=-1,
    )
    big = chip_pair_fold(total)
    small_at = half + third
    up_at = small_at + 128
    out_end = up_at + ff_half
    qkv_parts = [jnp.concatenate([p[:, :half], p[:, 2 * half : small_at]], axis=1) for p in big]
    down_halves = [
        jnp.concatenate([p[:, out_end + k * half : out_end + (k + 1) * half] for k in range(4)])
        for p in big
    ]
    down_part = rejoined(down_halves, 0, half)
    summed = (
        rejoined(qkv_parts, 0, third),
        rejoined(big, half, 2 * half),
        rejoined(big, up_at, out_end),
        down_part,
        (big[0] + big[1])[:, small_at : small_at + 12].reshape(-1),
    )
    qkv_new = adam_update(
        qkv_weight, qkv_moment, qkv_square, summed[0], MATRIX_RATE, MATRIX_DECAY, STEP
    )
    out_new = adam_update(
        out_weight, out_moment, out_square, summed[1], MATRIX_RATE, MATRIX_DECAY, STEP
    )
    up_new = adam_update(
        up_weight, up_moment, up_square, summed[2], MATRIX_RATE, MATRIX_DECAY, STEP
    )
    down_new = adam_update(
        down_weight, down_moment, down_square, summed[3], MATRIX_RATE, MATRIX_DECAY, STEP
    )
    small_new = adam_update(
        small_params, small_moment, small_square, summed[4], SMALL_RATE, 0.0, STEP
    )
    return (
        layer_out[None],
        input_grad[None],
        qkv_new[0],
        qkv_new[1],
        qkv_new[2],
        out_new[0],
        out_new[1],
        out_new[2],
        up_new[0],
        up_new[1],
        up_new[2],
        down_new[0],
        down_new[1],
        down_new[2],
        small_new[0],
        small_new[1],
        small_new[2],
    )


def solution(mesh):
    axes = ("xh", "z", "y", "c", "s")
    mesh = Mesh(mesh.devices.reshape(2, 4, 4, 2, 2), axes)
    return jax.shard_map(
        local,
        mesh=mesh,
        in_specs=(
            P(axes[:4], "s", None),
            P(axes[:4], "s"),
            P(axes[:4], "s", None),
            P(axes, None),
            P(axes, None),
            P(axes, None),
            P(axes, None),
            P(axes, None),
            P(axes, None),
            P(axes, None),
            P(axes, None),
            P(axes, None),
            P(axes, None),
            P(axes, None),
            P(axes, None),
            P(axes),
            P(axes),
            P(axes),
        ),
        out_specs=(
            P(axes[:4], "s", None),
            P(axes[:4], "s", None),
            P(axes, None),
            P(axes, None),
            P(axes, None),
            P(axes, None),
            P(axes, None),
            P(axes, None),
            P(axes, None),
            P(axes, None),
            P(axes, None),
            P(axes, None),
            P(axes, None),
            P(axes, None),
            P(axes),
            P(axes),
            P(axes),
        ),
        check_vma=False,
    )
```

```python
import functools
import math

import jax
import jax.numpy as jnp
from jax import lax
from jax.experimental import pallas as pl
from jax.experimental.pallas import tpu as pltpu
from jax.sharding import Mesh
from jax.sharding import PartitionSpec as P

HEADS = 12
STEP = 10


NORM_EPS = 1e-05
BETA_ONE = 0.9
BETA_TWO = 0.999
ADAM_EPS = 1e-08
MATRIX_RATE = 0.03
MATRIX_DECAY = 0.01
SMALL_RATE = 0.3
MASKED = -1e30
GELU_SCALE = math.sqrt(2.0 / math.pi)
GELU_CUBE = 0.044715
VMEM_SPARE = 6 * 1024 * 1024

BF16 = jnp.bfloat16
F32 = jnp.float32


def shifted_by(value, axis, steps):
    count = lax.axis_size(axis)
    return lax.ppermute(value, axis, [(k, (k + steps) % count) for k in range(count)])


def swapped(value, axes):
    count = lax.axis_size(axes)
    return lax.ppermute(value, axes, [(k, count - 1 - k) for k in range(count)])


def ring_pieces(value, axis):
    return [value] + [shifted_by(value, axis, r) for r in range(1, lax.axis_size(axis))]


def placed(pieces, axis, dim):
    count = len(pieces)
    me = lax.axis_index(axis)
    shape = list(pieces[0].shape)
    shape.insert(dim, count)
    total = jnp.zeros(shape, pieces[0].dtype)
    for r, piece in enumerate(pieces):
        total = lax.dynamic_update_index_in_dim(total, piece, (me - r) % count, dim)
    return total


def half_of(value, which):
    width = value.shape[-1] // 2
    return lax.dynamic_slice_in_dim(value, which * width, width, value.ndim - 1)


def pair_parts(keep, other):
    return keep, swapped(keep, "s"), swapped(other, "c"), swapped(other, ("c", "s"))


def together(*groups):
    return lax.optimization_barrier(groups)


def gather_start(first, last, visitors):
    width = first.shape[1] * 2 // 5
    first, last, visitors = together(
        ring_pieces(first, "y"), ring_pieces(last, "xh"), swapped(visitors, "s")
    )
    first = placed(first, "y", 0)
    one, two, last = first[..., :width], first[..., width:], placed(last, "xh", 0)
    one, two, last = together(one, two, last)
    one, two, last = together(ring_pieces(one, "z"), ring_pieces(two, "xh"), last)
    one, two = placed(one, "z", 0), placed(two, "xh", 0)
    return (*together(one, two, last), visitors)


def fold(terms, axis, dim, start=0, stop=None):
    count, me = lax.axis_size(axis), lax.axis_index(axis)
    blocks = []
    for r in range(count):
        parts = []
        for t in terms:
            at = [0] * t.ndim
            at[dim], at[-1] = (me + r) % count, start
            sizes = list(t.shape)
            sizes[dim], sizes[-1] = 1, (stop or t.shape[-1]) - start
            parts.append(jnp.squeeze(lax.dynamic_slice(t, at, sizes), dim))
        blocks.append(sum(p.astype(jnp.float32) for p in parts).astype(jnp.bfloat16))
    return blocks


def sent(blocks, axis):
    return [blocks[0]] + [shifted_by(blocks[r], axis, r) for r in range(1, len(blocks))]


def over_core(keep, send):
    shape = (2, 4, 4, keep.shape[0] // 32, keep.shape[1])
    return [keep.reshape(shape), swapped(send, "c").reshape(shape)]


def chip_pair_fold(total):
    core, side = lax.axis_index("c"), lax.axis_index("s")
    total = total.reshape((2, 2, total.shape[0] // 4) + total.shape[1:])

    def rows_of(k):
        at = ((core + k // 2) % 2, (side + k % 2) % 2) + (0,) * (total.ndim - 2)
        return lax.dynamic_slice(total, at, (1, 1) + total.shape[2:])[0, 0]

    def arrived(k, axes):
        return swapped(rows_of(k).astype(jnp.bfloat16), axes).astype(jnp.float32)

    mine = rows_of(0) + arrived(1, "s")
    theirs = arrived(2, "c") + arrived(3, ("c", "s"))
    return mine, theirs


def rejoined(pair, start, stop):
    core = lax.axis_index("c")
    mine, theirs = pair[0][:, start:stop], pair[1][:, start:stop]
    return jnp.concatenate(
        [jnp.where(core == 0, mine, theirs), jnp.where(core == 0, theirs, mine)], axis=1
    )


def adam_update(master, moment, square, gradient, step_rate, decay_rate, step_count):
    moment_new = BETA_ONE * moment + (1.0 - BETA_ONE) * gradient
    square_new = BETA_TWO * square + (1.0 - BETA_TWO) * gradient * gradient
    moment_hat = moment_new / (1.0 - BETA_ONE**step_count)
    square_hat = square_new / (1.0 - BETA_TWO**step_count)
    master_new = master - step_rate * (
        moment_hat / (jnp.sqrt(square_hat) + ADAM_EPS) + decay_rate * master
    )
    return (master_new, moment_new, square_new)


def dot_nn(left, right):
    return jnp.dot(left, right, preferred_element_type=F32)


def dot_nt(left, right):
    return lax.dot_general(left, right, (((1,), (1,)), ((), ())), preferred_element_type=F32)


def turned(values):
    return values.astype(F32).T


def lanes(start, size):
    return pl.ds(pl.multiple_of(start, 128), size)


def rows(start, size):
    return pl.ds(pl.multiple_of(start, size), size)


def weights_of(place_ref, axis, pieces, mine_ref, theirs_ref):
    count = len(pieces) // 2
    inner = pieces[0].shape[0]
    size = pieces[0].shape[1]
    for target, group in ((mine_ref, pieces[:count]), (theirs_ref, pieces[count:])):
        for r, piece in enumerate(group):
            at = lax.rem(place_ref[axis] - r + count, count)
            for part in range(inner):
                target[rows((part * count + at) * size, size), :] = piece[part]


def fetched(place_ref, axis, pieces, mine_ref, theirs_ref, sems):
    count = len(pieces) // 2
    inner, size = pieces[0].shape[:2]
    copies = []
    for target, group in ((mine_ref, pieces[:count]), (theirs_ref, pieces[count:])):
        for r, piece in enumerate(group):
            at = lax.rem(place_ref[axis] - r + count, count)
            for part in range(inner):
                copies.append(
                    pltpu.make_async_copy(
                        piece.at[part],
                        target.at[rows((part * count + at) * size, size), :],
                        sems.at[len(copies)],
                    )
                )
    for copy in copies:
        copy.start()
    return copies


def column_sum(values):
    return jnp.sum(values, axis=0, keepdims=True)


def line_masks(width, lane_count):
    per_row = 12
    group = width // per_row
    place = lax.broadcasted_iota(jnp.int32, (group, width), 1)
    row = lax.broadcasted_iota(jnp.int32, (group, width), 0)
    lane = lax.broadcasted_iota(jnp.int32, (width, lane_count), 1)
    start = lax.broadcasted_iota(jnp.int32, (width, lane_count), 0)
    inside = (place >= row * per_row) & (place < (row + 1) * per_row)
    pick = jnp.where(lax.rem(start, per_row) == lane, 1.0, 0.0).astype(BF16)
    return inside, pick


def norm_parts(values):
    center = values - jnp.mean(values, axis=-1, keepdims=True)
    spread = jnp.mean(center * center, axis=-1, keepdims=True)
    inverse = lax.rsqrt(spread + NORM_EPS)
    return center * inverse, inverse


def norm_pull(grad, hat, inverse, gain):
    scaled = gain * grad
    shift = jnp.mean(scaled, axis=-1, keepdims=True)
    slope = jnp.mean(scaled * hat, axis=-1, keepdims=True)
    return (scaled - shift - hat * slope) * inverse


def pack_kernel(place_ref, qkv_ref, small_ref, up_ref, out_ref, down_ref, keep_ref, other_ref):
    core = place_ref[0]
    for which, target in ((core, keep_ref), (1 - core, other_ref)):
        at = 0
        for source in (qkv_ref, small_ref, up_ref, out_ref):
            if source is small_ref:
                inside, pick = line_masks(source.shape[1], 128)
                line = jnp.where(inside, source[...], 0.0).astype(BF16)
                target[:, at : at + 128] = dot_nn(line, pick).astype(BF16)
                at += 128
                continue
            half = source.shape[1] // 2
            target[:, at : at + half] = source[:, lanes(which * half, half)].astype(BF16)
            at += half
        half = down_ref.shape[1] // 2
        count = target.shape[0]
        for part in range(down_ref.shape[0] // count):
            block = down_ref[part * count : (part + 1) * count, lanes(which * half, half)]
            target[:, at : at + half] = block.astype(BF16)
            at += half


def unpack_kernel(place_ref, *refs):
    parts, (first_ref, last_ref) = refs[:4], refs[4:]
    me = 2 * place_ref[0] + place_ref[1]
    count = parts[0].shape[0]
    width, half = first_ref.shape[1], last_ref.shape[1]
    values = [part[...].astype(F32) for part in parts]
    rows_first, rows_last = [], []
    for t in range(4):
        value = values[0]
        for k in range(1, 4):
            value = jnp.where(me == t ^ k, values[k], value)
        rows_first.append(value[:, :width])
        for at in range(width, value.shape[1], half):
            rows_last.append(value[:, at : at + half])
    first_ref[...] = jnp.concatenate(rows_first, axis=0).astype(BF16)
    last_ref[...] = jnp.concatenate(rows_last, axis=0).astype(BF16)


def segment_bias(own_ref, before_ref, late, width):
    own = own_ref.shape[0]
    total = 2 * own
    seg_own = own_ref[:, width:].astype(F32)
    seg_before = before_ref[:, width:].astype(F32)
    seg_before = jnp.where(late > 0, seg_before, -1.0)
    seg_k = jnp.concatenate([seg_before[:, 0:1], seg_own[:, 0:1]], axis=0)
    place_q = lax.broadcasted_iota(jnp.int32, (total, own), 1) + own
    place_k = lax.broadcasted_iota(jnp.int32, (total, own), 0)
    allowed = (seg_k == seg_own.T[0:1]) & (place_k <= place_q)
    return jnp.where(allowed, 0.0, MASKED)


def attend_kernel(core_ref, own_ref, before_ref, *refs):
    pieces = refs[:4]
    (
        turned_ref, q_ref, k_ref, v_ref, ctx_ref, ctx_turned_ref, lse_ref, vec_ref,
        normed_ref, proj_ref, bias_ref, mine_ref, theirs_ref,
    ) = refs[4:]
    weights_of(core_ref, 2, pieces, mine_ref, theirs_ref)
    core = core_ref[0]
    span = mine_ref.shape[1] - 128
    inside, pick = line_masks(q_ref.shape[1], 128)
    group = inside.shape[0]
    for r in range(vec_ref.shape[0]):
        lines = dot_nt(mine_ref[r * group : (r + 1) * group, span:], pick)
        vec_ref[r : r + 1, :] = column_sum(jnp.where(inside, lines, 0.0))
    own, width = q_ref.shape
    total = 2 * own
    half = proj_ref.shape[1] // 2
    tile = 384

    for source, base in ((before_ref, 0), (own_ref, own)):
        for part in range(0, own, 128):
            hat, _ = norm_parts(source[part : part + 128, :width].astype(F32))
            normed = hat * vec_ref[0:1, :] + vec_ref[1:2, :]
            normed_ref[base + part : base + part + 128, :] = normed.astype(BF16)
            turned_ref[:, base + part : base + part + 128] = turned(normed).astype(BF16)

    def proj_step(t, carry):
        normed = normed_ref[...]
        proj_ref[:, lanes(core * half + t * tile, tile)] = dot_nn(
            normed, mine_ref[:, lanes(t * tile, tile)]
        )
        proj_ref[:, lanes((1 - core) * half + t * tile, tile)] = dot_nn(
            normed, theirs_ref[:, lanes(t * tile, tile)]
        )
        return carry

    lax.fori_loop(0, half // tile, proj_step, 0)

    bias_ref[...] = segment_bias(own_ref, before_ref, core_ref[1], width)
    lane_row = lax.broadcasted_iota(jnp.int32, (1, 128), 1)

    def pair_step(j, carry):
        at = lanes(j * 128, 128)
        q = (proj_ref[total - own :, at] + vec_ref[2:3, at]).astype(BF16)
        k = proj_ref[:, lanes(width + j * 128, 128)].astype(BF16)
        v = (proj_ref[:, lanes(2 * width + j * 128, 128)] + vec_ref[3:4, at]).astype(BF16)
        q_ref[:, at] = q
        k_ref[:, at] = k
        v_ref[:, at] = v
        v_turned = turned(v).astype(BF16)
        outs = []
        for h in range(2):
            head_lanes = jnp.where(lane_row // 64 == h, 1.0, 0.0).astype(BF16)
            scores = dot_nt(k, q * head_lanes) * 0.125 + bias_ref[...]
            top = jnp.max(scores, axis=0, keepdims=True)
            weights = jnp.exp(scores - top)
            mass = jnp.sum(weights, axis=0, keepdims=True)
            probs = (weights * (1.0 / mass)).astype(BF16)
            outs.append(dot_nn(v_turned[h * 64 : (h + 1) * 64], probs))
            lse_ref[pl.ds(2 * j + h, 1), :] = top + jnp.log(mass)
        mixed = jnp.concatenate(outs, axis=0)
        ctx_turned_ref[rows(j * 128, 128), :] = mixed.astype(BF16)
        ctx_ref[:, at] = mixed.T.astype(BF16)
        return carry

    lax.fori_loop(0, HEADS // 2, pair_step, 0)


def up_kernel(
    core_ref, hid_ref, ctx_ref, vec_ref, *refs
):
    pieces = refs[:8]
    (
        mid_ref, turned_ref, act_ref, act_turned_ref, slope_ref,
        normed_ref, mine_ref, theirs_ref,
    ) = refs[8:]
    weights_of(core_ref, 3, pieces, mine_ref, theirs_ref)
    core = core_ref[0]
    width = hid_ref.shape[1]
    ff_half = act_ref.shape[1] // 2
    half = width // 2
    tile = 512
    ctx = ctx_ref[...]
    for which, ref in ((core, mine_ref), (1 - core, theirs_ref)):
        at = lanes(which * half, half)
        mid_ref[:, at] = (
            hid_ref[:, at].astype(F32)
            + (dot_nn(ctx, ref[:, ff_half : ff_half + half]) + vec_ref[4:5, at])
        )
    hat, _ = norm_parts(mid_ref[...])
    normed = hat * vec_ref[5:6, :] + vec_ref[6:7, :]
    normed_ref[...] = normed.astype(BF16)
    turned_ref[...] = turned(normed).astype(BF16)

    def up_step(t, carry):
        for which, ref in ((core, mine_ref), (1 - core, theirs_ref)):
            base = which * ff_half + t * tile
            pre = dot_nn(normed_ref[...], ref[:, lanes(t * tile, tile)])
            for part in range(tile // 256):
                at = base + part * 256
                u = pre[:, part * 256 : (part + 1) * 256] + vec_ref[
                    pl.ds(8 + at // width, 1), lanes(at % width, 256)
                ]
                square = u * u
                tanh = jnp.tanh(GELU_SCALE * (u + GELU_CUBE * (square * u)))
                act = 0.5 * u * (1.0 + tanh)
                act_ref[:, lanes(at, 256)] = act.astype(BF16)
                act_turned_ref[rows(at, 256), :] = turned(act).astype(BF16)
                slope_ref[:, lanes(at, 256)] = 0.5 * (1.0 + tanh) + (0.5 * GELU_SCALE) * u * (
                    1.0 - tanh * tanh
                ) * (1.0 + (3.0 * GELU_CUBE) * square)
        return carry

    lax.fori_loop(0, ff_half // tile, up_step, 0)


def down_kernel(core_ref, act_ref, grad_ref, keep_ref, send_ref):
    core = core_ref[0]
    half = grad_ref.shape[1] // 2
    tile = 512
    grads = jnp.concatenate(
        [grad_ref[:, lanes(core * half, half)], grad_ref[:, lanes((1 - core) * half, half)]], axis=1
    )

    def down_step(t, carry):
        at = rows(t * tile, tile)
        both = dot_nn(act_ref[at, :], grads).astype(BF16)
        keep_ref[at, :] = both[:, :half]
        send_ref[at, :] = both[:, half:]
        return carry

    lax.fori_loop(0, act_ref.shape[0] // tile, down_step, 0)


def middle_kernel(
    core_ref, normed_ref, slope_ref, grad_ref, *refs
):
    pieces = refs[:8]
    dpre_ref, send_ref, small_ref, down_mine_ref, down_theirs_ref = refs[8:]
    weights_of(core_ref, 4, pieces, down_mine_ref, down_theirs_ref)
    core = core_ref[0]
    width = normed_ref.shape[0]
    ff_half = slope_ref.shape[1] // 2
    half = width // 2
    tile = 512
    sides = ((core, down_mine_ref), (1 - core, down_theirs_ref))

    small_ref[0:1, :] = column_sum(grad_ref[...].astype(F32))

    def pre_step(t, carry):
        at = t * 256
        grad_act = sum(
            dot_nt(grad_ref[:, lanes(which * half, half)], down[rows(at, 256), :])
            for which, down in sides
        )
        pre = (grad_act * slope_ref[:, lanes(at, 256)]).astype(BF16)
        dpre_ref[:, lanes(at, 256)] = pre
        small_ref[pl.ds(1 + at // width, 1), lanes(at % width, 256)] = column_sum(pre.astype(F32))
        return carry

    lax.fori_loop(0, 2 * ff_half // 256, pre_step, 0)

    def weight_step(t, carry):
        pre = dpre_ref[:, lanes((1 - core) * ff_half + t * tile, tile)]
        send_ref[:, lanes(t * tile, tile)] = dot_nn(normed_ref[...], pre).astype(BF16)
        return carry

    lax.fori_loop(0, ff_half // tile, weight_step, 0)


def keep_kernel(core_ref, normed_ref, dpre_ref, keep_ref):
    core = core_ref[0]
    ff_half = dpre_ref.shape[1] // 2
    tile = 512

    def weight_step(t, carry):
        pre = dpre_ref[:, lanes(core * ff_half + t * tile, tile)]
        keep_ref[:, lanes(t * tile, tile)] = dot_nn(normed_ref[...], pre).astype(BF16)
        return carry

    lax.fori_loop(0, ff_half // tile, weight_step, 0)


def output_kernel(core_ref, mid_ref, act_ref, vec_ref, *refs):
    pieces = refs[:8]
    out_ref, mine_ref, theirs_ref = refs[8:]
    weights_of(core_ref, 4, pieces, mine_ref, theirs_ref)
    core = core_ref[0]
    half = mid_ref.shape[1] // 2
    for which, down in ((core, mine_ref), (1 - core, theirs_ref)):
        at = lanes(which * half, half)
        out_ref[:, at] = (
            mid_ref[:, at] + dot_nn(act_ref[...], down[...]) + vec_ref[7:8, at]
        ).astype(BF16)


def context_kernel(
    core_ref, mid_ref, grad_ref, ctx_ref, vec_ref, dpre_ref, *refs
):
    pieces = refs[:8]
    dmid_ref, dctx_ref, keep_ref, send_ref, small_ref, work_ref, mine_ref, theirs_ref = refs[8:]
    weights_of(core_ref, 3, pieces, mine_ref, theirs_ref)
    core = core_ref[0]
    width = mid_ref.shape[1]
    ff_half = dpre_ref.shape[1] // 2
    half = width // 2
    sides = ((core, mine_ref, keep_ref), (1 - core, theirs_ref, send_ref))

    def back_step(t, carry):
        at = t * 256
        work_ref[:, lanes(at, 256)] = sum(
            dot_nt(dpre_ref[:, lanes(which * ff_half, ff_half)], up[rows(at, 256), :ff_half])
            for which, up, _ in sides
        )
        return carry

    lax.fori_loop(0, width // 256, back_step, 0)

    grad_normed = work_ref[...]
    hat, inverse = norm_parts(mid_ref[...])
    small_ref[1:2, :] = column_sum(grad_normed * hat)
    small_ref[2:3, :] = column_sum(grad_normed)
    dmid = grad_ref[...].astype(F32) + norm_pull(grad_normed, hat, inverse, vec_ref[5:6, :])
    dmid_ref[...] = dmid
    small_ref[0:1, :] = column_sum(dmid.astype(BF16).astype(F32))

    ctx = ctx_ref[...]
    for which, _, target in sides:
        datt = dmid_ref[:, lanes(which * half, half)].astype(BF16)
        target[...] = dot_nn(ctx, datt).astype(BF16)

    def ctx_step(t, carry):
        at = t * 256
        dctx_ref[:, lanes(at, 256)] = sum(
            dot_nt(
                dmid_ref[:, lanes(which * half, half)].astype(BF16),
                out[rows(at, 256), ff_half : ff_half + half],
            )
            for which, out, _ in sides
        ).astype(BF16)
        return carry

    lax.fori_loop(0, width // 256, ctx_step, 0)


def first_kernel(
    core_ref, own_ref, before_ref,
    normed_ref, q_ref, k_ref, v_ref, lse_ref, dctx_ref,
    dproj_ref, send_ref, small_ref, bias_ref,
):
    core = core_ref[0]
    own, width = q_ref.shape
    total = normed_ref.shape[1]
    half = dproj_ref.shape[1] // 2
    tile = 384
    early = total - own

    bias_ref[...] = segment_bias(own_ref, before_ref, core_ref[1], width)
    dproj_ref[:early, :width] = jnp.zeros((early, width), BF16)
    lane_row = lax.broadcasted_iota(jnp.int32, (1, 128), 1)

    def pair_step(j, carry):
        at = lanes(j * 128, 128)
        q, k, v, dctx = q_ref[:, at], k_ref[:, at], v_ref[:, at], dctx_ref[:, at]
        k_turned = turned(k).astype(BF16)
        grad_q, grad_k, grad_v = [], [], []
        for h in range(2):
            head_lanes = jnp.where(lane_row // 64 == h, 1.0, 0.0).astype(BF16)
            q_head, dctx_head = q * head_lanes, dctx * head_lanes
            lse = lse_ref[pl.ds(2 * j + h, 1), :]
            probs = jnp.exp(dot_nt(k, q_head) * 0.125 + bias_ref[...] - lse)
            grad_probs = dot_nt(v, dctx_head)
            weighted = jnp.sum(probs * grad_probs, axis=0, keepdims=True)
            grad_scores = (probs * (grad_probs - weighted)).astype(BF16) * jnp.asarray(0.125, BF16)
            grad_q.append(dot_nn(k_turned[h * 64 : (h + 1) * 64], grad_scores))
            grad_k.append(dot_nn(grad_scores, q_head))
            grad_v.append(dot_nn(probs.astype(BF16), dctx_head))
        dq = jnp.concatenate(grad_q, axis=0).T.astype(BF16)
        dv = (grad_v[0] + grad_v[1]).astype(BF16)
        dproj_ref[early:, at] = dq
        dproj_ref[:, lanes(width + j * 128, 128)] = (grad_k[0] + grad_k[1]).astype(BF16)
        dproj_ref[:, lanes(2 * width + j * 128, 128)] = dv
        small_ref[0:1, at] = column_sum(dq.astype(F32))
        small_ref[1:2, at] = column_sum(dv.astype(F32))
        return carry

    lax.fori_loop(0, HEADS // 2, pair_step, 0)

    def weight_step(t, carry):
        normed = normed_ref[...]
        grads = dproj_ref[:, lanes((1 - core) * half + t * tile, tile)]
        send_ref[:, lanes(t * tile, tile)] = dot_nn(normed, grads).astype(BF16)
        return carry

    lax.fori_loop(0, half // tile, weight_step, 0)


def token_kernel(
    core_ref, own_ref, visit_ref, vec_ref, normed_ref, dproj_ref, dmid_ref, qv_ref, mid_small_ref,
    ff_small_ref, *refs
):
    pieces = refs[:4]
    (
        keep_ref, base_ref, before_ref, lines_ref,
        work_ref, mine_ref, theirs_ref, small_ref, spread_ref, sems,
    ) = refs[4:]
    copies = fetched(core_ref, 2, pieces, mine_ref, theirs_ref, sems)
    core = core_ref[0]
    own, width = base_ref.shape
    early = own
    half = dproj_ref.shape[1] // 2
    sides = ((core, mine_ref), (1 - core, theirs_ref))
    tile = 384

    def weight_step(t, carry):
        grads = dproj_ref[:, lanes(core * half + t * tile, tile)]
        keep_ref[:, lanes(t * tile, tile)] = dot_nn(normed_ref[...], grads).astype(BF16)
        return carry

    lax.fori_loop(0, half // tile, weight_step, 0)

    for copy in copies:
        copy.wait()

    def back_step(t, carry):
        at = t * 256
        work_ref[:, lanes(at, 256)] = sum(
            dot_nt(dproj_ref[:, lanes(which * half, half)], weight[rows(at, 256), :half])
            for which, weight in sides
        )
        return carry

    lax.fori_loop(0, width // 256, back_step, 0)

    grad_early = work_ref[:early, :]
    hat_early, _ = norm_parts(visit_ref[:, :width].astype(F32))
    before_ref[...] = grad_early.astype(BF16)
    grad_own = work_ref[early:, :]
    hat_own, inverse = norm_parts(own_ref[:, :width].astype(F32))
    small_ref[0:1, :] = column_sum(grad_early * hat_early) + column_sum(grad_own * hat_own)
    small_ref[1:2, :] = column_sum(grad_early) + column_sum(grad_own)
    base_ref[...] = dmid_ref[...] + norm_pull(grad_own, hat_own, inverse, vec_ref[0:1, :])
    at = 2
    for source in (qv_ref, mid_small_ref, ff_small_ref):
        small_ref[at : at + source.shape[0], :] = source[...]
        at += source.shape[0]
    inside, pick = line_masks(width, 128)
    group = inside.shape[0]
    for r in range(at):
        line = jnp.where(inside, small_ref[r : r + 1, :], 0.0)
        spread_ref[r * group : (r + 1) * group, :] = line.astype(BF16)
    lines_ref[...] = dot_nn(spread_ref[...], pick).astype(BF16)


def last_kernel(hid_ref, base_ref, later_ref, vec_ref, out_ref):
    hat, inverse = norm_parts(hid_ref[...].astype(F32))
    later = norm_pull(later_ref[...].astype(F32), hat, inverse, vec_ref[0:1, :])
    out_ref[...] = (base_ref[...] + later).astype(BF16)


def run(kernel, core, operands, outs, scratch=(), flops=0, name=None, moved=None, near=True, loose=0):
    whole = pl.BlockSpec(memory_space=pltpu.VMEM)
    moved = moved or sum(a.size * a.dtype.itemsize for a in operands)
    specs = [whole] * len(operands)
    room = sum(math.prod(shape) * jnp.dtype(dtype).itemsize for shape, dtype in scratch)
    buffers = [pltpu.VMEM(shape, dtype) for shape, dtype in scratch]
    if loose:
        specs[-loose:] = [pl.BlockSpec(memory_space=pltpu.HBM)] * loose
        buffers.append(pltpu.SemaphoreType.DMA((loose * operands[-1].shape[0],)))
    if near:
        shapes = [pltpu.VMEM(shape, dtype) for shape, dtype in outs]
        operands = [
            pltpu.with_memory_space_constraint(
                a, pltpu.VMEM if k < len(operands) - loose else pltpu.HBM
            )
            for k, a in enumerate(operands)
        ]
    else:
        shapes = [jax.ShapeDtypeStruct(shape, dtype) for shape, dtype in outs]
        operands = [pltpu.with_memory_space_constraint(a, pltpu.HBM) for a in operands]
        room += sum(a.size * a.dtype.itemsize for a in (*operands, *shapes))
    if core is not None:
        operands = (core, *operands)
        specs = [pl.BlockSpec(memory_space=pltpu.SMEM)] + specs
    return pl.pallas_call(
        kernel,
        out_shape=shapes,
        in_specs=specs,
        out_specs=[whole] * len(shapes),
        scratch_shapes=buffers,
        compiler_params=pltpu.CompilerParams(vmem_limit_bytes=room + VMEM_SPARE),
        cost_estimate=pl.CostEstimate(flops=flops, bytes_accessed=moved, transcendentals=0),
        name=name,
    )(*operands)


def local(
    hidden_in,
    segment_ids,
    out_cotangent,
    qkv_weight,
    qkv_moment,
    qkv_square,
    out_weight,
    out_moment,
    out_square,
    up_weight,
    up_moment,
    up_square,
    down_weight,
    down_moment,
    down_square,
    small_params,
    small_moment,
    small_square,
):
    width = out_weight.shape[1]
    hidden = up_weight.shape[1]
    half, ff_half, third = width // 2, hidden // 2, qkv_weight.shape[1] // 2
    own = hidden_in.shape[1]
    tokens, upstream, seg_own = hidden_in[0], out_cotangent[0], segment_ids[0]
    core = lax.axis_index("c")

    place = jnp.stack([lax.axis_index(a) for a in ("c", "s", "xh", "z", "y")]).astype(jnp.int32)

    def shaped(pieces, inner):
        return [p.reshape(inner, -1, p.shape[-1]) for p in pieces]

    span = third + 128 + ff_half + half
    keep, other = run(
        pack_kernel,
        place,
        (qkv_weight, small_params.reshape(1, -1), up_weight, out_weight, down_weight),
        [((6, span + 4 * half), BF16)] * 2,
        near=False,
        name="pack",
    )
    first, last = run(
        unpack_kernel,
        place,
        pair_parts(keep, other),
        [((24, span), BF16), ((96, half), BF16)],
        name="unpack",
    )
    first, last, tokens_in, seg_in = together(first, last, tokens, seg_own)
    seg_line = jnp.broadcast_to(seg_in.astype(BF16)[:, None], (own, 128))
    own_lines = jnp.concatenate([tokens_in, seg_line], axis=1)
    one, two, last, visitors = gather_start(first, last, own_lines)

    one = ring_pieces(one, "xh")
    two = [two] + [shifted_by(two, "z", r) for r in (1, 3)]
    one_first, two_first = swapped(one[0], "c"), swapped(two[0], "c")
    one_first, last = together(one_first, last)
    last = ring_pieces(last, "z")
    one, one_first, two, two_first, last = together(one, one_first, two, two_first, last)
    last = placed(last, "z", 1)
    one_theirs = swapped(one[1], "c")
    two_theirs = [two_first, swapped(two[1], "c"), swapped(two[2], "c")]
    one_theirs, two_theirs, last, two = together(one_theirs, two_theirs, last, two)
    last_near = [shifted_by(last, "y", r) for r in (1, 3)]
    last_far = shifted_by(last, "y", 2)
    two_far = shifted_by(two[0], "z", 2)
    one = shaped(one + [one_first, one_theirs], 1)

    normed_one, queries, keys, values, context, context_turned, lse, vectors = run(
        attend_kernel,
        place,
        (own_lines, visitors, *one),
        [
            ((width, 2 * own), BF16), ((own, width), BF16), ((2 * own, width), BF16),
            ((2 * own, width), BF16), ((own, width), BF16), ((width, own), BF16),
            ((16, own), F32), ((12, width), F32),
        ],
        [
            ((2 * own, width), BF16),
            ((2 * own, 3 * width), F32), ((2 * own, own), F32),
            ((width, third + 128), BF16), ((width, third + 128), BF16),
        ],
        flops=12_000_000_000,
        name="attend",
    )
    context, lse, two_far, last_near = together(context, lse, two_far, last_near)
    two = shaped(
        [two[0], two[1], two_far, two[2]]
        + [two_theirs[0], two_theirs[1], swapped(two_far, "c"), two_theirs[2]],
        2,
    )
    middle, normed_two, activated, act_turned, slope = run(
        up_kernel,
        place,
        (tokens, context, vectors, *two),
        [
            ((own, width), F32), ((width, own), BF16), ((own, hidden), BF16),
            ((hidden, own), BF16), ((own, hidden), F32),
        ],
        [((own, width), BF16), ((width, ff_half + half), BF16), ((width, ff_half + half), BF16)],
        flops=1_000,
        moved=1_000,
        name="up",
    )
    last_theirs = [swapped(p, "c") for p in (last, *last_near)]
    middle, act_turned, last_far, last_theirs = together(
        middle, act_turned, last_far, last_theirs
    )
    far_theirs = swapped(last_far, "c")
    down_keep, down_send = run(
        down_kernel,
        place,
        (act_turned, upstream),
        [((hidden, half), BF16), ((hidden, half), BF16)],
        flops=3_000_000_000,
        name="down",
    )
    down_keep, down_send, far_theirs = together(down_keep, down_send, far_theirs)
    last = [
        last, last_near[0], last_far, last_near[1],
        last_theirs[0], last_theirs[1], far_theirs, last_theirs[2],
    ]
    last = shaped(together(*last), 8)
    fold_down = over_core(down_keep, down_send)
    grad_pre, up_send, small_mid = run(
        middle_kernel,
        place,
        (normed_two, slope, upstream, *last),
        [((own, hidden), BF16), ((width, ff_half), BF16), ((5, width), F32)],
        [((hidden, half), BF16), ((hidden, half), BF16)],
        flops=9_000_000_000,
        name="middle",
    )
    grad_pre, up_send, fold_down = together(grad_pre, up_send, fold_down)
    up_theirs = swapped(up_send, "c")
    blocks_down = fold(fold_down, "y", 2)
    grad_pre, blocks_down = together(grad_pre, blocks_down)
    sent_down = sent(blocks_down, "y")
    (up_keep,) = run(
        keep_kernel,
        place,
        (normed_two, grad_pre),
        [((width, ff_half), BF16)],
        flops=2_500_000_000,
        name="keep",
    )
    up_keep, up_theirs, grad_pre = together(up_keep, up_theirs, grad_pre)
    shape = (2, 4, 4, -1, ff_half)
    blocks_two = fold([up_keep.reshape(shape), up_theirs.reshape(shape)], "z", 1)
    blocks_two, grad_pre = together(blocks_two, grad_pre)
    two_near = [shifted_by(blocks_two[r], "z", r) for r in (1, 3)]
    grad_middle, grad_context, out_keep, out_send, small_ctx = run(
        context_kernel,
        place,
        (middle, upstream, context_turned, vectors, grad_pre, *two),
        [
            ((own, width), F32), ((own, width), BF16), ((width, half), BF16),
            ((width, half), BF16), ((3, width), F32),
        ],
        [
            ((own, width), F32), ((width, ff_half + half), BF16),
            ((width, ff_half + half), BF16),
        ],
        flops=9_000_000_000,
        name="context",
    )
    activated, grad_middle = together(activated, grad_middle)
    (layer_out,) = run(
        output_kernel,
        place,
        (middle, activated, vectors, *last),
        [((own, width), BF16)],
        [((hidden, half), BF16), ((hidden, half), BF16)],
        flops=3_000_000_000,
        name="output",
    )
    (
        grad_middle, grad_context, out_keep, out_send, sent_down, two_near, two_far, layer_out
    ) = together(
        grad_middle, grad_context, out_keep, out_send, sent_down, two_near, blocks_two[2], layer_out
    )
    fold_out = over_core(out_keep, out_send)
    blocks_down = fold(sent_down, "xh", 0)
    blocks_down, grad_context = together(blocks_down, grad_context)
    two_far = shifted_by(two_far, "z", 2)
    sent_down = sent(blocks_down, "xh")
    grad_proj, one_send, small_qv = run(
        first_kernel,
        place,
        (own_lines, visitors, normed_one, queries, keys, values, lse, grad_context),
        [((2 * own, 3 * width), BF16), ((width, third), BF16), ((2, width), F32)],
        [((2 * own, own), F32)],
        flops=15_000_000_000,
        name="first",
    )
    grad_proj, one_send, two_far, sent_down, fold_out = together(
        grad_proj, one_send, two_far, sent_down, fold_out
    )
    one_theirs = swapped(one_send, "c")
    blocks_two = fold([blocks_two[0], two_near[0], two_far, two_near[1]], "xh", 0)
    blocks_down = fold(sent_down, "z", 0)
    blocks_two, blocks_down, grad_proj = together(blocks_two, blocks_down, grad_proj)
    sent_two, sent_down = sent(blocks_two, "xh"), sent(blocks_down, "z")
    one_keep, base, before, small_lines = run(
        token_kernel,
        place,
        (
            own_lines, visitors, vectors, normed_one, grad_proj, grad_middle,
            small_qv, small_ctx, small_mid, *one,
        ),
        [
            ((width, third), BF16), ((own, width), F32), ((own, width), BF16),
            ((width, 128), BF16),
        ],
        [
            ((2 * own, width), F32), ((width, third + 128), BF16), ((width, third + 128), BF16),
            ((12, width), F32), ((width, width), BF16),
        ],
        flops=8_000_000_000,
        loose=4,
        name="token",
    )
    one_keep, one_theirs, small_lines, before, sent_down, sent_two = together(
        one_keep, one_theirs, small_lines, before, sent_down, sent_two
    )
    shape = (2, 4, 4, -1, third)
    fold_one = [one_keep.reshape(shape), one_theirs.reshape(shape)]
    small_lines = small_lines.reshape(2, 4, 4, -1, 128)
    cut = half
    blocks_left = [
        jnp.concatenate(b, axis=-1)
        for b in zip(fold(fold_one, "xh", 0, 0, cut), fold(fold_out, "xh", 0))
    ]
    blocks_right = [
        jnp.concatenate(b, axis=-1)
        for b in zip(fold(fold_one, "y", 2, cut), fold([small_lines], "y", 2))
    ]
    blocks_left, blocks_right = together(blocks_left, blocks_right)
    sent_left, sent_right = sent(blocks_left, "xh"), sent(blocks_right, "y")
    sent_left, sent_right = together(sent_left, sent_right)
    later = lax.ppermute(before, "s", [(1, 0)])
    sent_left = sent(fold(sent_left, "y", 1), "y")
    sent_right = sent(fold(sent_right, "xh", 0), "xh")
    sent_left, sent_right, later = together(sent_left, sent_right, later)
    blocks_one = [
        jnp.concatenate(b, axis=-1)
        for b in zip(fold(sent_left, "z", 0), fold(sent_right, "z", 0))
    ]
    sent_one = sent(blocks_one, "z")
    sent_two = sent(fold(sent_two, "y", 0), "y")
    (input_grad,) = run(
        last_kernel,
        None,
        (tokens, base, later, vectors),
        [((own, width), BF16)],
        flops=100_000_000,
        near=False,
        name="last",
    )
    sent_one, sent_two, input_grad = together(sent_one, sent_two, input_grad)
    down_total = sum(t.astype(F32) for t in sent_down).reshape(4, 4, 6, half)
    down_total = jnp.concatenate([down_total[:, k] for k in range(4)], axis=-1)
    total = jnp.concatenate(
        [sum(t.astype(F32) for t in g) for g in (sent_one, sent_two)]
        + [down_total.reshape(24, 4 * half)],
        axis=-1,
    )
    big = chip_pair_fold(total)
    small_at = half + third
    up_at = small_at + 128
    out_end = up_at + ff_half
    qkv_parts = [jnp.concatenate([p[:, :half], p[:, 2 * half : small_at]], axis=1) for p in big]
    down_halves = [
        jnp.concatenate([p[:, out_end + k * half : out_end + (k + 1) * half] for k in range(4)])
        for p in big
    ]
    down_part = rejoined(down_halves, 0, half)
    summed = (
        rejoined(qkv_parts, 0, third),
        rejoined(big, half, 2 * half),
        rejoined(big, up_at, out_end),
        down_part,
        (big[0] + big[1])[:, small_at : small_at + 12].reshape(-1),
    )
    qkv_new = adam_update(
        qkv_weight, qkv_moment, qkv_square, summed[0], MATRIX_RATE, MATRIX_DECAY, STEP
    )
    out_new = adam_update(
        out_weight, out_moment, out_square, summed[1], MATRIX_RATE, MATRIX_DECAY, STEP
    )
    up_new = adam_update(
        up_weight, up_moment, up_square, summed[2], MATRIX_RATE, MATRIX_DECAY, STEP
    )
    down_new = adam_update(
        down_weight, down_moment, down_square, summed[3], MATRIX_RATE, MATRIX_DECAY, STEP
    )
    small_new = adam_update(
        small_params, small_moment, small_square, summed[4], SMALL_RATE, 0.0, STEP
    )
    return (
        layer_out[None],
        input_grad[None],
        qkv_new[0],
        qkv_new[1],
        qkv_new[2],
        out_new[0],
        out_new[1],
        out_new[2],
        up_new[0],
        up_new[1],
        up_new[2],
        down_new[0],
        down_new[1],
        down_new[2],
        small_new[0],
        small_new[1],
        small_new[2],
    )


def solution(mesh):
    axes = ("xh", "z", "y", "c", "s")
    mesh = Mesh(mesh.devices.reshape(2, 4, 4, 2, 2), axes)
    return jax.shard_map(
        local,
        mesh=mesh,
        in_specs=(
            P(axes[:4], "s", None),
            P(axes[:4], "s"),
            P(axes[:4], "s", None),
            P(axes, None),
            P(axes, None),
            P(axes, None),
            P(axes, None),
            P(axes, None),
            P(axes, None),
            P(axes, None),
            P(axes, None),
            P(axes, None),
            P(axes, None),
            P(axes, None),
            P(axes, None),
            P(axes),
            P(axes),
            P(axes),
        ),
        out_specs=(
            P(axes[:4], "s", None),
            P(axes[:4], "s", None),
            P(axes, None),
            P(axes, None),
            P(axes, None),
            P(axes, None),
            P(axes, None),
            P(axes, None),
            P(axes, None),
            P(axes, None),
            P(axes, None),
            P(axes, None),
            P(axes, None),
            P(axes, None),
            P(axes),
            P(axes),
            P(axes),
        ),
        check_vma=False,
    )
```

```python
import functools
import math

import jax
import jax.numpy as jnp
from jax import lax
from jax.experimental import pallas as pl
from jax.experimental.pallas import tpu as pltpu
from jax.sharding import Mesh
from jax.sharding import PartitionSpec as P

HEADS = 12
STEP = 10


NORM_EPS = 1e-05
BETA_ONE = 0.9
BETA_TWO = 0.999
ADAM_EPS = 1e-08
MATRIX_RATE = 0.03
MATRIX_DECAY = 0.01
SMALL_RATE = 0.3
MASKED = -1e30
GELU_SCALE = math.sqrt(2.0 / math.pi)
GELU_CUBE = 0.044715
VMEM_SPARE = 6 * 1024 * 1024

BF16 = jnp.bfloat16
F32 = jnp.float32


def shifted_by(value, axis, steps):
    count = lax.axis_size(axis)
    return lax.ppermute(value, axis, [(k, (k + steps) % count) for k in range(count)])


def swapped(value, axes):
    count = lax.axis_size(axes)
    return lax.ppermute(value, axes, [(k, count - 1 - k) for k in range(count)])


def ring_pieces(value, axis):
    return [value] + [shifted_by(value, axis, r) for r in range(1, lax.axis_size(axis))]


def placed(pieces, axis, dim):
    count = len(pieces)
    me = lax.axis_index(axis)
    shape = list(pieces[0].shape)
    shape.insert(dim, count)
    total = jnp.zeros(shape, pieces[0].dtype)
    for r, piece in enumerate(pieces):
        total = lax.dynamic_update_index_in_dim(total, piece, (me - r) % count, dim)
    return total


def half_of(value, which):
    width = value.shape[-1] // 2
    return lax.dynamic_slice_in_dim(value, which * width, width, value.ndim - 1)


def pair_parts(keep, other):
    return keep, swapped(keep, "s"), swapped(other, "c"), swapped(other, ("c", "s"))


def together(*groups):
    return lax.optimization_barrier(groups)


def gather_start(first, last, visitors):
    width = first.shape[1] * 2 // 5
    first, last, visitors = together(
        ring_pieces(first, "y"), ring_pieces(last, "xh"), swapped(visitors, "s")
    )
    first = placed(first, "y", 0)
    one, two, last = first[..., :width], first[..., width:], placed(last, "xh", 0)
    one, two, last = together(one, two, last)
    one, two, last = together(ring_pieces(one, "z"), ring_pieces(two, "xh"), last)
    one, two = placed(one, "z", 0), placed(two, "xh", 0)
    return (*together(one, two, last), visitors)


def fold(terms, axis, dim, start=0, stop=None):
    count, me = lax.axis_size(axis), lax.axis_index(axis)
    blocks = []
    for r in range(count):
        parts = []
        for t in terms:
            at = [0] * t.ndim
            at[dim], at[-1] = (me + r) % count, start
            sizes = list(t.shape)
            sizes[dim], sizes[-1] = 1, (stop or t.shape[-1]) - start
            parts.append(jnp.squeeze(lax.dynamic_slice(t, at, sizes), dim))
        blocks.append(sum(p.astype(jnp.float32) for p in parts).astype(jnp.bfloat16))
    return blocks


def sent(blocks, axis):
    return [blocks[0]] + [shifted_by(blocks[r], axis, r) for r in range(1, len(blocks))]


def over_core(keep, send):
    shape = (2, 4, 4, keep.shape[0] // 32, keep.shape[1])
    return [keep.reshape(shape), swapped(send, "c").reshape(shape)]


def chip_pair_fold(total):
    core, side = lax.axis_index("c"), lax.axis_index("s")
    total = total.reshape((2, 2, total.shape[0] // 4) + total.shape[1:])

    def rows_of(k):
        at = ((core + k // 2) % 2, (side + k % 2) % 2) + (0,) * (total.ndim - 2)
        return lax.dynamic_slice(total, at, (1, 1) + total.shape[2:])[0, 0]

    def arrived(k, axes):
        return swapped(rows_of(k).astype(jnp.bfloat16), axes).astype(jnp.float32)

    mine = rows_of(0) + arrived(1, "s")
    theirs = arrived(2, "c") + arrived(3, ("c", "s"))
    return mine, theirs


def rejoined(pair, start, stop):
    core = lax.axis_index("c")
    mine, theirs = pair[0][:, start:stop], pair[1][:, start:stop]
    return jnp.concatenate(
        [jnp.where(core == 0, mine, theirs), jnp.where(core == 0, theirs, mine)], axis=1
    )


def adam_update(master, moment, square, gradient, step_rate, decay_rate, step_count):
    moment_new = BETA_ONE * moment + (1.0 - BETA_ONE) * gradient
    square_new = BETA_TWO * square + (1.0 - BETA_TWO) * gradient * gradient
    moment_hat = moment_new / (1.0 - BETA_ONE**step_count)
    square_hat = square_new / (1.0 - BETA_TWO**step_count)
    master_new = master - step_rate * (
        moment_hat / (jnp.sqrt(square_hat) + ADAM_EPS) + decay_rate * master
    )
    return (master_new, moment_new, square_new)


def dot_nn(left, right):
    return jnp.dot(left, right, preferred_element_type=F32)


def dot_nt(left, right):
    return lax.dot_general(left, right, (((1,), (1,)), ((), ())), preferred_element_type=F32)


def turned(values):
    return values.astype(F32).T


def lanes(start, size):
    return pl.ds(pl.multiple_of(start, 128), size)


def rows(start, size):
    return pl.ds(pl.multiple_of(start, size), size)


def weights_of(place_ref, axis, pieces, mine_ref, theirs_ref):
    count = len(pieces) // 2
    inner = pieces[0].shape[0]
    size = pieces[0].shape[1]
    for target, group in ((mine_ref, pieces[:count]), (theirs_ref, pieces[count:])):
        for r, piece in enumerate(group):
            at = lax.rem(place_ref[axis] - r + count, count)
            for part in range(inner):
                target[rows((part * count + at) * size, size), :] = piece[part]


def fetched(place_ref, axis, pieces, mine_ref, theirs_ref, sems):
    count = len(pieces) // 2
    inner, size = pieces[0].shape[:2]
    copies = []
    for target, group in ((mine_ref, pieces[:count]), (theirs_ref, pieces[count:])):
        for r, piece in enumerate(group):
            at = lax.rem(place_ref[axis] - r + count, count)
            for part in range(inner):
                copies.append(
                    pltpu.make_async_copy(
                        piece.at[part],
                        target.at[rows((part * count + at) * size, size), :],
                        sems.at[len(copies)],
                    )
                )
    for copy in copies:
        copy.start()
    return copies


def column_sum(values):
    return jnp.sum(values, axis=0, keepdims=True)


def line_masks(width, lane_count):
    per_row = 12
    group = width // per_row
    place = lax.broadcasted_iota(jnp.int32, (group, width), 1)
    row = lax.broadcasted_iota(jnp.int32, (group, width), 0)
    lane = lax.broadcasted_iota(jnp.int32, (width, lane_count), 1)
    start = lax.broadcasted_iota(jnp.int32, (width, lane_count), 0)
    inside = (place >= row * per_row) & (place < (row + 1) * per_row)
    pick = jnp.where(lax.rem(start, per_row) == lane, 1.0, 0.0).astype(BF16)
    return inside, pick


def norm_parts(values):
    center = values - jnp.mean(values, axis=-1, keepdims=True)
    spread = jnp.mean(center * center, axis=-1, keepdims=True)
    inverse = lax.rsqrt(spread + NORM_EPS)
    return center * inverse, inverse


def norm_pull(grad, hat, inverse, gain):
    scaled = gain * grad
    shift = jnp.mean(scaled, axis=-1, keepdims=True)
    slope = jnp.mean(scaled * hat, axis=-1, keepdims=True)
    return (scaled - shift - hat * slope) * inverse


def pack_kernel(place_ref, qkv_ref, small_ref, up_ref, out_ref, down_ref, keep_ref, other_ref):
    core = place_ref[0]
    for which, target in ((core, keep_ref), (1 - core, other_ref)):
        at = 0
        for source in (qkv_ref, small_ref, up_ref, out_ref):
            if source is small_ref:
                inside, pick = line_masks(source.shape[1], 128)
                line = jnp.where(inside, source[...], 0.0).astype(BF16)
                target[:, at : at + 128] = dot_nn(line, pick).astype(BF16)
                at += 128
                continue
            half = source.shape[1] // 2
            target[:, at : at + half] = source[:, lanes(which * half, half)].astype(BF16)
            at += half
        half = down_ref.shape[1] // 2
        count = target.shape[0]
        for part in range(down_ref.shape[0] // count):
            block = down_ref[part * count : (part + 1) * count, lanes(which * half, half)]
            target[:, at : at + half] = block.astype(BF16)
            at += half


def unpack_kernel(place_ref, *refs):
    parts, (first_ref, last_ref) = refs[:4], refs[4:]
    me = 2 * place_ref[0] + place_ref[1]
    count = parts[0].shape[0]
    width, half = first_ref.shape[1], last_ref.shape[1]
    values = [part[...].astype(F32) for part in parts]
    rows_first, rows_last = [], []
    for t in range(4):
        value = values[0]
        for k in range(1, 4):
            value = jnp.where(me == t ^ k, values[k], value)
        rows_first.append(value[:, :width])
        for at in range(width, value.shape[1], half):
            rows_last.append(value[:, at : at + half])
    first_ref[...] = jnp.concatenate(rows_first, axis=0).astype(BF16)
    last_ref[...] = jnp.concatenate(rows_last, axis=0).astype(BF16)


def segment_bias(own_ref, before_ref, late, width):
    own = own_ref.shape[0]
    total = 2 * own
    seg_own = own_ref[:, width:].astype(F32)
    seg_before = before_ref[:, width:].astype(F32)
    seg_before = jnp.where(late > 0, seg_before, -1.0)
    seg_k = jnp.concatenate([seg_before[:, 0:1], seg_own[:, 0:1]], axis=0)
    place_q = lax.broadcasted_iota(jnp.int32, (total, own), 1) + own
    place_k = lax.broadcasted_iota(jnp.int32, (total, own), 0)
    allowed = (seg_k == seg_own.T[0:1]) & (place_k <= place_q)
    return jnp.where(allowed, 0.0, MASKED)


def attend_kernel(core_ref, own_ref, before_ref, *refs):
    pieces = refs[:4]
    (
        turned_ref, q_ref, k_ref, v_ref, ctx_ref, ctx_turned_ref, lse_ref, vec_ref,
        normed_ref, proj_ref, bias_ref, mine_ref, theirs_ref,
    ) = refs[4:]
    weights_of(core_ref, 2, pieces, mine_ref, theirs_ref)
    core = core_ref[0]
    span = mine_ref.shape[1] - 128
    inside, pick = line_masks(q_ref.shape[1], 128)
    group = inside.shape[0]
    for r in range(vec_ref.shape[0]):
        lines = dot_nt(mine_ref[r * group : (r + 1) * group, span:], pick)
        vec_ref[r : r + 1, :] = column_sum(jnp.where(inside, lines, 0.0))
    own, width = q_ref.shape
    total = 2 * own
    half = proj_ref.shape[1] // 2
    tile = 384

    for source, base in ((before_ref, 0), (own_ref, own)):
        for part in range(0, own, 128):
            hat, _ = norm_parts(source[part : part + 128, :width].astype(F32))
            normed = hat * vec_ref[0:1, :] + vec_ref[1:2, :]
            normed_ref[base + part : base + part + 128, :] = normed.astype(BF16)
            turned_ref[:, base + part : base + part + 128] = turned(normed).astype(BF16)

    def proj_step(t, carry):
        normed = normed_ref[...]
        proj_ref[:, lanes(core * half + t * tile, tile)] = dot_nn(
            normed, mine_ref[:, lanes(t * tile, tile)]
        )
        proj_ref[:, lanes((1 - core) * half + t * tile, tile)] = dot_nn(
            normed, theirs_ref[:, lanes(t * tile, tile)]
        )
        return carry

    lax.fori_loop(0, half // tile, proj_step, 0)

    bias_ref[...] = segment_bias(own_ref, before_ref, core_ref[1], width)
    lane_row = lax.broadcasted_iota(jnp.int32, (1, 128), 1)

    def pair_step(j, carry):
        at = lanes(j * 128, 128)
        q = (proj_ref[total - own :, at] + vec_ref[2:3, at]).astype(BF16)
        k = proj_ref[:, lanes(width + j * 128, 128)].astype(BF16)
        v = (proj_ref[:, lanes(2 * width + j * 128, 128)] + vec_ref[3:4, at]).astype(BF16)
        q_ref[:, at] = q
        k_ref[:, at] = k
        v_ref[:, at] = v
        v_turned = turned(v).astype(BF16)
        outs = []
        for h in range(2):
            head_lanes = jnp.where(lane_row // 64 == h, 1.0, 0.0).astype(BF16)
            scores = dot_nt(k, q * head_lanes) * 0.125 + bias_ref[...]
            top = jnp.max(scores, axis=0, keepdims=True)
            weights = jnp.exp(scores - top)
            mass = jnp.sum(weights, axis=0, keepdims=True)
            probs = (weights * (1.0 / mass)).astype(BF16)
            outs.append(dot_nn(v_turned[h * 64 : (h + 1) * 64], probs))
            lse_ref[pl.ds(2 * j + h, 1), :] = top + jnp.log(mass)
        mixed = jnp.concatenate(outs, axis=0)
        ctx_turned_ref[rows(j * 128, 128), :] = mixed.astype(BF16)
        ctx_ref[:, at] = mixed.T.astype(BF16)
        return carry

    lax.fori_loop(0, HEADS // 2, pair_step, 0)


def up_kernel(
    core_ref, hid_ref, ctx_ref, vec_ref, *refs
):
    pieces = refs[:8]
    (
        mid_ref, turned_ref, act_ref, act_turned_ref, slope_ref,
        normed_ref, mine_ref, theirs_ref,
    ) = refs[8:]
    weights_of(core_ref, 3, pieces, mine_ref, theirs_ref)
    core = core_ref[0]
    width = hid_ref.shape[1]
    ff_half = act_ref.shape[1] // 2
    half = width // 2
    tile = 512
    ctx = ctx_ref[...]
    for which, ref in ((core, mine_ref), (1 - core, theirs_ref)):
        at = lanes(which * half, half)
        mid_ref[:, at] = (
            hid_ref[:, at].astype(F32)
            + (dot_nn(ctx, ref[:, ff_half : ff_half + half]) + vec_ref[4:5, at])
        )
    hat, _ = norm_parts(mid_ref[...])
    normed = hat * vec_ref[5:6, :] + vec_ref[6:7, :]
    normed_ref[...] = normed.astype(BF16)
    turned_ref[...] = turned(normed).astype(BF16)

    def up_step(t, carry):
        for which, ref in ((core, mine_ref), (1 - core, theirs_ref)):
            base = which * ff_half + t * tile
            pre = dot_nn(normed_ref[...], ref[:, lanes(t * tile, tile)])
            for part in range(tile // 256):
                at = base + part * 256
                u = pre[:, part * 256 : (part + 1) * 256] + vec_ref[
                    pl.ds(8 + at // width, 1), lanes(at % width, 256)
                ]
                square = u * u
                tanh = jnp.tanh(GELU_SCALE * (u + GELU_CUBE * (square * u)))
                act = 0.5 * u * (1.0 + tanh)
                act_ref[:, lanes(at, 256)] = act.astype(BF16)
                act_turned_ref[rows(at, 256), :] = turned(act).astype(BF16)
                slope_ref[:, lanes(at, 256)] = 0.5 * (1.0 + tanh) + (0.5 * GELU_SCALE) * u * (
                    1.0 - tanh * tanh
                ) * (1.0 + (3.0 * GELU_CUBE) * square)
        return carry

    lax.fori_loop(0, ff_half // tile, up_step, 0)


def down_kernel(core_ref, act_ref, grad_ref, keep_ref, send_ref):
    core = core_ref[0]
    half = grad_ref.shape[1] // 2
    tile = 512
    grads = jnp.concatenate(
        [grad_ref[:, lanes(core * half, half)], grad_ref[:, lanes((1 - core) * half, half)]], axis=1
    )

    def down_step(t, carry):
        at = rows(t * tile, tile)
        both = dot_nn(act_ref[at, :], grads).astype(BF16)
        keep_ref[at, :] = both[:, :half]
        send_ref[at, :] = both[:, half:]
        return carry

    lax.fori_loop(0, act_ref.shape[0] // tile, down_step, 0)


def middle_kernel(
    core_ref, normed_ref, slope_ref, grad_ref, *refs
):
    pieces = refs[:8]
    dpre_ref, send_ref, small_ref, down_mine_ref, down_theirs_ref = refs[8:]
    weights_of(core_ref, 4, pieces, down_mine_ref, down_theirs_ref)
    core = core_ref[0]
    width = normed_ref.shape[0]
    ff_half = slope_ref.shape[1] // 2
    half = width // 2
    tile = 512
    sides = ((core, down_mine_ref), (1 - core, down_theirs_ref))

    small_ref[0:1, :] = column_sum(grad_ref[...].astype(F32))

    def pre_step(t, carry):
        at = t * 256
        grad_act = sum(
            dot_nt(grad_ref[:, lanes(which * half, half)], down[rows(at, 256), :])
            for which, down in sides
        )
        pre = (grad_act * slope_ref[:, lanes(at, 256)]).astype(BF16)
        dpre_ref[:, lanes(at, 256)] = pre
        small_ref[pl.ds(1 + at // width, 1), lanes(at % width, 256)] = column_sum(pre.astype(F32))
        return carry

    lax.fori_loop(0, 2 * ff_half // 256, pre_step, 0)

    def weight_step(t, carry):
        pre = dpre_ref[:, lanes((1 - core) * ff_half + t * tile, tile)]
        send_ref[:, lanes(t * tile, tile)] = dot_nn(normed_ref[...], pre).astype(BF16)
        return carry

    lax.fori_loop(0, ff_half // tile, weight_step, 0)


def keep_kernel(core_ref, normed_ref, dpre_ref, keep_ref):
    core = core_ref[0]
    ff_half = dpre_ref.shape[1] // 2
    tile = 512

    def weight_step(t, carry):
        pre = dpre_ref[:, lanes(core * ff_half + t * tile, tile)]
        keep_ref[:, lanes(t * tile, tile)] = dot_nn(normed_ref[...], pre).astype(BF16)
        return carry

    lax.fori_loop(0, ff_half // tile, weight_step, 0)


def output_kernel(core_ref, mid_ref, act_ref, vec_ref, *refs):
    pieces = refs[:8]
    out_ref, mine_ref, theirs_ref = refs[8:]
    weights_of(core_ref, 4, pieces, mine_ref, theirs_ref)
    core = core_ref[0]
    half = mid_ref.shape[1] // 2
    for which, down in ((core, mine_ref), (1 - core, theirs_ref)):
        at = lanes(which * half, half)
        out_ref[:, at] = (
            mid_ref[:, at] + dot_nn(act_ref[...], down[...]) + vec_ref[7:8, at]
        ).astype(BF16)


def context_kernel(
    core_ref, mid_ref, grad_ref, ctx_ref, vec_ref, dpre_ref, *refs
):
    pieces = refs[:8]
    dmid_ref, dctx_ref, keep_ref, send_ref, small_ref, work_ref, mine_ref, theirs_ref = refs[8:]
    weights_of(core_ref, 3, pieces, mine_ref, theirs_ref)
    core = core_ref[0]
    width = mid_ref.shape[1]
    ff_half = dpre_ref.shape[1] // 2
    half = width // 2
    sides = ((core, mine_ref, keep_ref), (1 - core, theirs_ref, send_ref))

    def back_step(t, carry):
        at = t * 256
        work_ref[:, lanes(at, 256)] = sum(
            dot_nt(dpre_ref[:, lanes(which * ff_half, ff_half)], up[rows(at, 256), :ff_half])
            for which, up, _ in sides
        )
        return carry

    lax.fori_loop(0, width // 256, back_step, 0)

    grad_normed = work_ref[...]
    hat, inverse = norm_parts(mid_ref[...])
    small_ref[1:2, :] = column_sum(grad_normed * hat)
    small_ref[2:3, :] = column_sum(grad_normed)
    dmid = grad_ref[...].astype(F32) + norm_pull(grad_normed, hat, inverse, vec_ref[5:6, :])
    dmid_ref[...] = dmid
    small_ref[0:1, :] = column_sum(dmid.astype(BF16).astype(F32))

    ctx = ctx_ref[...]
    for which, _, target in sides:
        datt = dmid_ref[:, lanes(which * half, half)].astype(BF16)
        target[...] = dot_nn(ctx, datt).astype(BF16)

    def ctx_step(t, carry):
        at = t * 256
        dctx_ref[:, lanes(at, 256)] = sum(
            dot_nt(
                dmid_ref[:, lanes(which * half, half)].astype(BF16),
                out[rows(at, 256), ff_half : ff_half + half],
            )
            for which, out, _ in sides
        ).astype(BF16)
        return carry

    lax.fori_loop(0, width // 256, ctx_step, 0)


def first_kernel(
    core_ref, own_ref, before_ref,
    normed_ref, q_ref, k_ref, v_ref, lse_ref, dctx_ref,
    dproj_ref, send_ref, small_ref, bias_ref,
):
    core = core_ref[0]
    own, width = q_ref.shape
    total = normed_ref.shape[1]
    half = dproj_ref.shape[1] // 2
    tile = 384
    early = total - own

    bias_ref[...] = segment_bias(own_ref, before_ref, core_ref[1], width)
    dproj_ref[:early, :width] = jnp.zeros((early, width), BF16)
    lane_row = lax.broadcasted_iota(jnp.int32, (1, 128), 1)

    def pair_step(j, carry):
        at = lanes(j * 128, 128)
        q, k, v, dctx = q_ref[:, at], k_ref[:, at], v_ref[:, at], dctx_ref[:, at]
        k_turned = turned(k).astype(BF16)
        grad_q, grad_k, grad_v = [], [], []
        for h in range(2):
            head_lanes = jnp.where(lane_row // 64 == h, 1.0, 0.0).astype(BF16)
            q_head, dctx_head = q * head_lanes, dctx * head_lanes
            lse = lse_ref[pl.ds(2 * j + h, 1), :]
            probs = jnp.exp(dot_nt(k, q_head) * 0.125 + bias_ref[...] - lse)
            grad_probs = dot_nt(v, dctx_head)
            weighted = jnp.sum(probs * grad_probs, axis=0, keepdims=True)
            grad_scores = (probs * (grad_probs - weighted)).astype(BF16) * jnp.asarray(0.125, BF16)
            grad_q.append(dot_nn(k_turned[h * 64 : (h + 1) * 64], grad_scores))
            grad_k.append(dot_nn(grad_scores, q_head))
            grad_v.append(dot_nn(probs.astype(BF16), dctx_head))
        dq = jnp.concatenate(grad_q, axis=0).T.astype(BF16)
        dv = (grad_v[0] + grad_v[1]).astype(BF16)
        dproj_ref[early:, at] = dq
        dproj_ref[:, lanes(width + j * 128, 128)] = (grad_k[0] + grad_k[1]).astype(BF16)
        dproj_ref[:, lanes(2 * width + j * 128, 128)] = dv
        small_ref[0:1, at] = column_sum(dq.astype(F32))
        small_ref[1:2, at] = column_sum(dv.astype(F32))
        return carry

    lax.fori_loop(0, HEADS // 2, pair_step, 0)

    def weight_step(t, carry):
        normed = normed_ref[...]
        grads = dproj_ref[:, lanes((1 - core) * half + t * tile, tile)]
        send_ref[:, lanes(t * tile, tile)] = dot_nn(normed, grads).astype(BF16)
        return carry

    lax.fori_loop(0, half // tile, weight_step, 0)


def token_kernel(
    core_ref, own_ref, visit_ref, vec_ref, normed_ref, dproj_ref, dmid_ref, qv_ref, mid_small_ref,
    ff_small_ref, *refs
):
    pieces = refs[:4]
    (
        keep_ref, base_ref, before_ref, lines_ref,
        work_ref, mine_ref, theirs_ref, small_ref, spread_ref, sems,
    ) = refs[4:]
    copies = fetched(core_ref, 2, pieces, mine_ref, theirs_ref, sems)
    core = core_ref[0]
    own, width = base_ref.shape
    early = own
    half = dproj_ref.shape[1] // 2
    sides = ((core, mine_ref), (1 - core, theirs_ref))
    tile = 384

    def weight_step(t, carry):
        grads = dproj_ref[:, lanes(core * half + t * tile, tile)]
        keep_ref[:, lanes(t * tile, tile)] = dot_nn(normed_ref[...], grads).astype(BF16)
        return carry

    lax.fori_loop(0, half // tile, weight_step, 0)

    for copy in copies:
        copy.wait()

    def back_step(t, carry):
        at = t * 256
        work_ref[:, lanes(at, 256)] = sum(
            dot_nt(dproj_ref[:, lanes(which * half, half)], weight[rows(at, 256), :half])
            for which, weight in sides
        )
        return carry

    lax.fori_loop(0, width // 256, back_step, 0)

    grad_early = work_ref[:early, :]
    hat_early, _ = norm_parts(visit_ref[:, :width].astype(F32))
    before_ref[...] = grad_early.astype(BF16)
    grad_own = work_ref[early:, :]
    hat_own, inverse = norm_parts(own_ref[:, :width].astype(F32))
    small_ref[0:1, :] = column_sum(grad_early * hat_early) + column_sum(grad_own * hat_own)
    small_ref[1:2, :] = column_sum(grad_early) + column_sum(grad_own)
    base_ref[...] = dmid_ref[...] + norm_pull(grad_own, hat_own, inverse, vec_ref[0:1, :])
    at = 2
    for source in (qv_ref, mid_small_ref, ff_small_ref):
        small_ref[at : at + source.shape[0], :] = source[...]
        at += source.shape[0]
    inside, pick = line_masks(width, 128)
    group = inside.shape[0]
    for r in range(at):
        line = jnp.where(inside, small_ref[r : r + 1, :], 0.0)
        spread_ref[r * group : (r + 1) * group, :] = line.astype(BF16)
    lines_ref[...] = dot_nn(spread_ref[...], pick).astype(BF16)


def last_kernel(hid_ref, base_ref, later_ref, vec_ref, out_ref):
    hat, inverse = norm_parts(hid_ref[...].astype(F32))
    later = norm_pull(later_ref[...].astype(F32), hat, inverse, vec_ref[0:1, :])
    out_ref[...] = (base_ref[...] + later).astype(BF16)


def run(kernel, core, operands, outs, scratch=(), flops=0, name=None, moved=None, near=True, loose=0):
    whole = pl.BlockSpec(memory_space=pltpu.VMEM)
    moved = moved or sum(a.size * a.dtype.itemsize for a in operands)
    specs = [whole] * len(operands)
    room = sum(math.prod(shape) * jnp.dtype(dtype).itemsize for shape, dtype in scratch)
    buffers = [pltpu.VMEM(shape, dtype) for shape, dtype in scratch]
    if loose:
        specs[-loose:] = [pl.BlockSpec(memory_space=pltpu.HBM)] * loose
        buffers.append(pltpu.SemaphoreType.DMA((loose * operands[-1].shape[0],)))
    if near:
        shapes = [pltpu.VMEM(shape, dtype) for shape, dtype in outs]
        operands = [
            pltpu.with_memory_space_constraint(
                a, pltpu.VMEM if k < len(operands) - loose else pltpu.HBM
            )
            for k, a in enumerate(operands)
        ]
    else:
        shapes = [jax.ShapeDtypeStruct(shape, dtype) for shape, dtype in outs]
        operands = [pltpu.with_memory_space_constraint(a, pltpu.HBM) for a in operands]
        room += sum(a.size * a.dtype.itemsize for a in (*operands, *shapes))
    if core is not None:
        operands = (core, *operands)
        specs = [pl.BlockSpec(memory_space=pltpu.SMEM)] + specs
    return pl.pallas_call(
        kernel,
        out_shape=shapes,
        in_specs=specs,
        out_specs=[whole] * len(shapes),
        scratch_shapes=buffers,
        compiler_params=pltpu.CompilerParams(vmem_limit_bytes=room + VMEM_SPARE),
        cost_estimate=pl.CostEstimate(flops=flops, bytes_accessed=moved, transcendentals=0),
        name=name,
    )(*operands)


def local(
    hidden_in,
    segment_ids,
    out_cotangent,
    qkv_weight,
    qkv_moment,
    qkv_square,
    out_weight,
    out_moment,
    out_square,
    up_weight,
    up_moment,
    up_square,
    down_weight,
    down_moment,
    down_square,
    small_params,
    small_moment,
    small_square,
):
    width = out_weight.shape[1]
    hidden = up_weight.shape[1]
    half, ff_half, third = width // 2, hidden // 2, qkv_weight.shape[1] // 2
    own = hidden_in.shape[1]
    tokens, upstream, seg_own = hidden_in[0], out_cotangent[0], segment_ids[0]
    core = lax.axis_index("c")

    place = jnp.stack([lax.axis_index(a) for a in ("c", "s", "xh", "z", "y")]).astype(jnp.int32)

    def shaped(pieces, inner):
        return [p.reshape(inner, -1, p.shape[-1]) for p in pieces]

    span = third + 128 + ff_half + half
    keep, other = run(
        pack_kernel,
        place,
        (qkv_weight, small_params.reshape(1, -1), up_weight, out_weight, down_weight),
        [((6, span + 4 * half), BF16)] * 2,
        near=False,
        name="pack",
    )
    first, last = run(
        unpack_kernel,
        place,
        pair_parts(keep, other),
        [((24, span), BF16), ((96, half), BF16)],
        name="unpack",
    )
    first, last, tokens_in, seg_in = together(first, last, tokens, seg_own)
    seg_line = jnp.broadcast_to(seg_in.astype(BF16)[:, None], (own, 128))
    own_lines = jnp.concatenate([tokens_in, seg_line], axis=1)
    one, two, last, visitors = gather_start(first, last, own_lines)

    one = ring_pieces(one, "xh")
    two = [two] + [shifted_by(two, "z", r) for r in (1, 3)]
    one_first, two_first = swapped(one[0], "c"), swapped(two[0], "c")
    one_first, last = together(one_first, last)
    last = ring_pieces(last, "z")
    one, one_first, two, two_first, last = together(one, one_first, two, two_first, last)
    last = placed(last, "z", 1)
    one_theirs = swapped(one[1], "c")
    two_theirs = [two_first, swapped(two[1], "c"), swapped(two[2], "c")]
    one_theirs, two_theirs, last, two = together(one_theirs, two_theirs, last, two)
    last_near = [shifted_by(last, "y", r) for r in (1, 3)]
    last_far = shifted_by(last, "y", 2)
    two_far = shifted_by(two[0], "z", 2)
    one = shaped(one + [one_first, one_theirs], 1)

    normed_one, queries, keys, values, context, context_turned, lse, vectors = run(
        attend_kernel,
        place,
        (own_lines, visitors, *one),
        [
            ((width, 2 * own), BF16), ((own, width), BF16), ((2 * own, width), BF16),
            ((2 * own, width), BF16), ((own, width), BF16), ((width, own), BF16),
            ((16, own), F32), ((12, width), F32),
        ],
        [
            ((2 * own, width), BF16),
            ((2 * own, 3 * width), F32), ((2 * own, own), F32),
            ((width, third + 128), BF16), ((width, third + 128), BF16),
        ],
        flops=12_000_000_000,
        name="attend",
    )
    context, lse, two_far, last_near, last_far = together(
        context, lse, two_far, last_near, last_far
    )
    two = shaped(
        [two[0], two[1], two_far, two[2]]
        + [two_theirs[0], two_theirs[1], swapped(two_far, "c"), two_theirs[2]],
        2,
    )
    middle, normed_two, activated, act_turned, slope = run(
        up_kernel,
        place,
        (tokens, context, vectors, *two),
        [
            ((own, width), F32), ((width, own), BF16), ((own, hidden), BF16),
            ((hidden, own), BF16), ((own, hidden), F32),
        ],
        [((own, width), BF16), ((width, ff_half + half), BF16), ((width, ff_half + half), BF16)],
        flops=6_000_000_000,
        name="up",
    )
    last_theirs = [swapped(p, "c") for p in (last, *last_near)]
    middle, act_turned, last_far, last_theirs = together(
        middle, act_turned, last_far, last_theirs
    )
    far_theirs = swapped(last_far, "c")
    down_keep, down_send = run(
        down_kernel,
        place,
        (act_turned, upstream),
        [((hidden, half), BF16), ((hidden, half), BF16)],
        flops=3_000_000_000,
        name="down",
    )
    down_keep, down_send, far_theirs = together(down_keep, down_send, far_theirs)
    last = [
        last, last_near[0], last_far, last_near[1],
        last_theirs[0], last_theirs[1], far_theirs, last_theirs[2],
    ]
    last = shaped(together(*last), 8)
    fold_down = over_core(down_keep, down_send)
    grad_pre, up_send, small_mid = run(
        middle_kernel,
        place,
        (normed_two, slope, upstream, *last),
        [((own, hidden), BF16), ((width, ff_half), BF16), ((5, width), F32)],
        [((hidden, half), BF16), ((hidden, half), BF16)],
        flops=9_000_000_000,
        name="middle",
    )
    grad_pre, up_send, fold_down = together(grad_pre, up_send, fold_down)
    up_theirs = swapped(up_send, "c")
    blocks_down = fold(fold_down, "y", 2)
    grad_pre, blocks_down = together(grad_pre, blocks_down)
    sent_down = sent(blocks_down, "y")
    (up_keep,) = run(
        keep_kernel,
        place,
        (normed_two, grad_pre),
        [((width, ff_half), BF16)],
        flops=2_500_000_000,
        name="keep",
    )
    up_keep, up_theirs, grad_pre = together(up_keep, up_theirs, grad_pre)
    shape = (2, 4, 4, -1, ff_half)
    blocks_two = fold([up_keep.reshape(shape), up_theirs.reshape(shape)], "z", 1)
    blocks_two, grad_pre = together(blocks_two, grad_pre)
    two_near = [shifted_by(blocks_two[r], "z", r) for r in (1, 3)]
    grad_middle, grad_context, out_keep, out_send, small_ctx = run(
        context_kernel,
        place,
        (middle, upstream, context_turned, vectors, grad_pre, *two),
        [
            ((own, width), F32), ((own, width), BF16), ((width, half), BF16),
            ((width, half), BF16), ((3, width), F32),
        ],
        [
            ((own, width), F32), ((width, ff_half + half), BF16),
            ((width, ff_half + half), BF16),
        ],
        flops=9_000_000_000,
        name="context",
    )
    activated, grad_middle = together(activated, grad_middle)
    (layer_out,) = run(
        output_kernel,
        place,
        (middle, activated, vectors, *last),
        [((own, width), BF16)],
        [((hidden, half), BF16), ((hidden, half), BF16)],
        flops=3_000_000_000,
        name="output",
    )
    (
        grad_middle, grad_context, out_keep, out_send, sent_down, two_near, two_far, layer_out
    ) = together(
        grad_middle, grad_context, out_keep, out_send, sent_down, two_near, blocks_two[2], layer_out
    )
    fold_out = over_core(out_keep, out_send)
    blocks_down = fold(sent_down, "xh", 0)
    blocks_down, grad_context = together(blocks_down, grad_context)
    two_far = shifted_by(two_far, "z", 2)
    sent_down = sent(blocks_down, "xh")
    grad_proj, one_send, small_qv = run(
        first_kernel,
        place,
        (own_lines, visitors, normed_one, queries, keys, values, lse, grad_context),
        [((2 * own, 3 * width), BF16), ((width, third), BF16), ((2, width), F32)],
        [((2 * own, own), F32)],
        flops=15_000_000_000,
        name="first",
    )
    grad_proj, one_send, two_far, sent_down, fold_out = together(
        grad_proj, one_send, two_far, sent_down, fold_out
    )
    one_theirs = swapped(one_send, "c")
    blocks_two = fold([blocks_two[0], two_near[0], two_far, two_near[1]], "xh", 0)
    blocks_down = fold(sent_down, "z", 0)
    blocks_two, blocks_down, grad_proj = together(blocks_two, blocks_down, grad_proj)
    sent_two, sent_down = sent(blocks_two, "xh"), sent(blocks_down, "z")
    one_keep, base, before, small_lines = run(
        token_kernel,
        place,
        (
            own_lines, visitors, vectors, normed_one, grad_proj, grad_middle,
            small_qv, small_ctx, small_mid, *one,
        ),
        [
            ((width, third), BF16), ((own, width), F32), ((own, width), BF16),
            ((width, 128), BF16),
        ],
        [
            ((2 * own, width), F32), ((width, third + 128), BF16), ((width, third + 128), BF16),
            ((12, width), F32), ((width, width), BF16),
        ],
        flops=8_000_000_000,
        loose=4,
        name="token",
    )
    one_keep, one_theirs, small_lines, before, sent_down, sent_two = together(
        one_keep, one_theirs, small_lines, before, sent_down, sent_two
    )
    shape = (2, 4, 4, -1, third)
    fold_one = [one_keep.reshape(shape), one_theirs.reshape(shape)]
    small_lines = small_lines.reshape(2, 4, 4, -1, 128)
    cut = half
    blocks_left = [
        jnp.concatenate(b, axis=-1)
        for b in zip(fold(fold_one, "xh", 0, 0, cut), fold(fold_out, "xh", 0))
    ]
    blocks_right = [
        jnp.concatenate(b, axis=-1)
        for b in zip(fold(fold_one, "y", 2, cut), fold([small_lines], "y", 2))
    ]
    blocks_left, blocks_right = together(blocks_left, blocks_right)
    sent_left, sent_right = sent(blocks_left, "xh"), sent(blocks_right, "y")
    sent_left, sent_right = together(sent_left, sent_right)
    later = lax.ppermute(before, "s", [(1, 0)])
    sent_left = sent(fold(sent_left, "y", 1), "y")
    sent_right = sent(fold(sent_right, "xh", 0), "xh")
    sent_left, sent_right, later = together(sent_left, sent_right, later)
    blocks_one = [
        jnp.concatenate(b, axis=-1)
        for b in zip(fold(sent_left, "z", 0), fold(sent_right, "z", 0))
    ]
    sent_one = sent(blocks_one, "z")
    sent_two = sent(fold(sent_two, "y", 0), "y")
    (input_grad,) = run(
        last_kernel,
        None,
        (tokens, base, later, vectors),
        [((own, width), BF16)],
        flops=100_000_000,
        near=False,
        name="last",
    )
    sent_one, sent_two, input_grad = together(sent_one, sent_two, input_grad)
    down_total = sum(t.astype(F32) for t in sent_down).reshape(4, 4, 6, half)
    down_total = jnp.concatenate([down_total[:, k] for k in range(4)], axis=-1)
    total = jnp.concatenate(
        [sum(t.astype(F32) for t in g) for g in (sent_one, sent_two)]
        + [down_total.reshape(24, 4 * half)],
        axis=-1,
    )
    big = chip_pair_fold(total)
    small_at = half + third
    up_at = small_at + 128
    out_end = up_at + ff_half
    qkv_parts = [jnp.concatenate([p[:, :half], p[:, 2 * half : small_at]], axis=1) for p in big]
    down_halves = [
        jnp.concatenate([p[:, out_end + k * half : out_end + (k + 1) * half] for k in range(4)])
        for p in big
    ]
    down_part = rejoined(down_halves, 0, half)
    summed = (
        rejoined(qkv_parts, 0, third),
        rejoined(big, half, 2 * half),
        rejoined(big, up_at, out_end),
        down_part,
        (big[0] + big[1])[:, small_at : small_at + 12].reshape(-1),
    )
    qkv_new = adam_update(
        qkv_weight, qkv_moment, qkv_square, summed[0], MATRIX_RATE, MATRIX_DECAY, STEP
    )
    out_new = adam_update(
        out_weight, out_moment, out_square, summed[1], MATRIX_RATE, MATRIX_DECAY, STEP
    )
    up_new = adam_update(
        up_weight, up_moment, up_square, summed[2], MATRIX_RATE, MATRIX_DECAY, STEP
    )
    down_new = adam_update(
        down_weight, down_moment, down_square, summed[3], MATRIX_RATE, MATRIX_DECAY, STEP
    )
    small_new = adam_update(
        small_params, small_moment, small_square, summed[4], SMALL_RATE, 0.0, STEP
    )
    return (
        layer_out[None],
        input_grad[None],
        qkv_new[0],
        qkv_new[1],
        qkv_new[2],
        out_new[0],
        out_new[1],
        out_new[2],
        up_new[0],
        up_new[1],
        up_new[2],
        down_new[0],
        down_new[1],
        down_new[2],
        small_new[0],
        small_new[1],
        small_new[2],
    )


def solution(mesh):
    axes = ("xh", "z", "y", "c", "s")
    mesh = Mesh(mesh.devices.reshape(2, 4, 4, 2, 2), axes)
    return jax.shard_map(
        local,
        mesh=mesh,
        in_specs=(
            P(axes[:4], "s", None),
            P(axes[:4], "s"),
            P(axes[:4], "s", None),
            P(axes, None),
            P(axes, None),
            P(axes, None),
            P(axes, None),
            P(axes, None),
            P(axes, None),
            P(axes, None),
            P(axes, None),
            P(axes, None),
            P(axes, None),
            P(axes, None),
            P(axes, None),
            P(axes),
            P(axes),
            P(axes),
        ),
        out_specs=(
            P(axes[:4], "s", None),
            P(axes[:4], "s", None),
            P(axes, None),
            P(axes, None),
            P(axes, None),
            P(axes, None),
            P(axes, None),
            P(axes, None),
            P(axes, None),
            P(axes, None),
            P(axes, None),
            P(axes, None),
            P(axes, None),
            P(axes, None),
            P(axes),
            P(axes),
            P(axes),
        ),
        check_vma=False,
    )
```
